512 devices in a mesh: vis: 16 (over z_lo, core), tp: 8 (over z_hi, x), dp: 4 (over y).
Axes of the slice: x: 4, y: 4, z: 16 (z_hi: 2, z_lo: 8; z = z_hi * 8 + z_lo), core: 2. Of those that a mesh axis runs over, the one named last changes fastest.
Arguments:
- features: bfloat16 [6144, 4, 1280], P('vis', 'dp'), may hold values from -6 to 6
- merge_weight: bfloat16 [4, 1280, 8192], P('dp', None, 'tp'), may hold values from -0.078125 to 0.078125
- gain: float32 [8192], P('tp'), may hold values from 0.1 to 1.9
- positions: int32 [6144], replicated, may hold values from 0 to 8191, as said below
- cotangent: bfloat16 [8192, 8192], P(('vis', 'dp'), 'tp'), may hold values from -6 to 6
Outputs:
- feature_grad: bfloat16 [6144, 4, 1280], P('vis', 'dp')
- weight_grad: bfloat16 [4, 1280, 8192], P('dp', 'vis', 'tp')
The draws below stay inside these ranges and needn't reach their ends.
Inputs may be any that keep to these rules, and one draw needn't show every extreme that they name: Positions are distinct. Split the rows into aligned blocks of 96 and the positions into owners' ranges of 128: each block sends exactly 2 rows to one owner and spreads the rest as evenly as possible over the other owners, in an order drawn at random.
All inputs are finite; a program needn't handle non-finite values.
Results may differ from the reference program's by a relative error of at most 0.023.
Values may be sent and summed in bfloat16 or wider, within the bound.
A program may use at most 64 MiB of HBM per device.

```python
import jax
import jax.numpy as jnp
from jax import lax

D = 8192
VIS_W = 1280
MERGE = 4
ROWS_VIS = 384
SLOTS_DEV = 128
CAP = 2
VROWS = 6144
TOKENS = 8192
N_VIS = 16
N_DP = 4


def draw_positions(key, part):
    key = jax.random.fold_in(key, 11)
    owners = N_VIS * N_DP
    per_block = ROWS_VIS // N_DP
    total = ROWS_VIS * N_VIS
    order_key, slot_key, first_key = jax.random.split(key, 3)
    leaders = jax.random.permutation(first_key, owners).astype(jnp.int32)
    rests = jax.vmap(lambda sub_key: jax.random.permutation(sub_key, owners - 1))(jax.random.split(order_key, owners)).astype(jnp.int32)
    others = (leaders[:, None] + 1 + rests) % owners
    orders = jnp.concatenate([leaders[:, None], others], axis=1)
    within = jnp.arange(per_block, dtype=jnp.int32)
    pick = jnp.where(within < CAP, 0, 1 + (within - CAP) % (owners - 1))
    owner_of = orders[:, pick].reshape(total).astype(jnp.int32)
    onehot = (owner_of[:, None] == jnp.arange(owners, dtype=jnp.int32)[None, :]).astype(jnp.int32)
    counted = jnp.cumsum(onehot, axis=0)
    rank_in = jnp.sum(counted * onehot, axis=1) - 1
    slot_tables = jax.vmap(lambda sub_key: jax.random.permutation(sub_key, SLOTS_DEV))(jax.random.split(slot_key, owners)).astype(jnp.int32)
    owner_ids = jnp.arange(owners, dtype=jnp.int32)
    wanted = jnp.where(owner_ids == owners - 1, SLOTS_DEV - 1, 0)
    shift_by = jnp.where((owner_ids == 0) | (owner_ids == owners - 1), wanted - slot_tables[:, 0], 0)
    slot_tables = (slot_tables + shift_by[:, None]) % SLOTS_DEV
    return (owner_of * SLOTS_DEV + slot_tables[owner_of, rank_in]).astype(jnp.int32)


def spiked(entries, stream_key, source, target, blocks, factor):
    def block_of(dim):
        return (jnp.arange(entries.shape[dim]) // (entries.shape[dim] // blocks)).reshape((-1,) + (1,) * (entries.ndim - 1 - dim))

    near = jax.random.permutation(stream_key, blocks)[block_of(target)]
    far = (block_of(target) + blocks // 2) % blocks
    return jnp.where((block_of(source) == near) | (block_of(source) == far), factor * entries, entries)


def level_of(key, dims, shards, smallest, largest):
    level = 1.0
    for axis_at, shards_of in shards:
        steps = jax.random.uniform(jax.random.fold_in(jax.random.fold_in(key, 6), axis_at), (shards_of,), jnp.float32, smallest / len(shards), largest / len(shards))
        level = level * jnp.repeat(jnp.exp(steps), dims[axis_at] // shards_of).reshape((-1,) + (1,) * (len(dims) - 1 - axis_at))
    return level


def bell_draw(rng, dims, scale, limit, shards=(), kind=jnp.bfloat16):
    loudness = level_of(rng, dims, shards, -0.22, 0.18) if shards else 1.0
    result = jax.random.normal(rng, dims, jnp.float32) * scale * loudness
    return jnp.minimum(jnp.maximum(result, -limit), limit).astype(kind)


def heavy_noise(stream_key, shape, width, reach, pieces, heavy, kind=jnp.bfloat16):
    values = width * jax.random.normal(stream_key, shape, jnp.float32)
    if pieces:
        values = values * level_of(stream_key, shape, pieces, -0.22, 0.18)
    return jnp.clip(spiked(values, jax.random.fold_in(stream_key, 3), *heavy), -reach, reach).astype(kind)


def setup_inputs(seed: int = 0) -> dict:
    splits = jax.random.split(jax.random.key(seed), 6)
    return {
        "features": heavy_noise(splits[0], (VROWS, MERGE, VIS_W), 1.0, 6.0, ((0, 16), (1, 4)), (0, 2, 16, 2.0)),
        "merge_weight": bell_draw(splits[1], (MERGE, VIS_W, D), (MERGE * VIS_W) ** -0.5, 0.078125, ((0, 4), (2, 8))),
        "gain": jnp.clip(1.0 + 0.18 * jax.random.normal(splits[2], (D,), jnp.float32), 0.1, 1.9),
        "positions": draw_positions(jax.random.fold_in(splits[5], 71), 0),
        "cotangent": bell_draw(splits[4], (TOKENS, D), 1.0, 6.0, ((0, 64), (1, 8))),
    }


eps = 1e-06

def norm_backward(rows, cot_rows, gain_full):
    values = rows.astype(jnp.float32)
    scaled = cot_rows.astype(jnp.float32) * gain_full[None, :]
    sq_sum = lax.optimization_barrier(jnp.sum(values * values, axis=1))
    dot_sum = lax.optimization_barrier(jnp.sum(scaled * values, axis=1))
    inverse = lax.rsqrt(sq_sum / D + eps)
    grad = inverse[:, None] * scaled - (inverse ** 3 * dot_sum / D)[:, None] * values
    return grad.astype(jnp.bfloat16)

def reference(features, merge_weight, gain, positions, cotangent):
    total = jnp.zeros((VROWS, D), jnp.float32)
    for sub in range(MERGE):
        term = jnp.dot(features[:, sub, :], merge_weight[sub], preferred_element_type=jnp.float32)
        rounded = lax.optimization_barrier(term.astype(jnp.bfloat16))
        total = total + rounded.astype(jnp.float32)
    vis_rows = total.astype(jnp.bfloat16)
    cot_rows = cotangent[positions]
    grad_rows = norm_backward(vis_rows, cot_rows, gain.astype(jnp.float32))
    columns = []
    for sub in range(MERGE):
        product = jnp.dot(grad_rows, merge_weight[sub].T, preferred_element_type=jnp.float32)
        columns.append(product.astype(jnp.bfloat16))
    feature_grad = jnp.stack(columns, axis=1)

    def add_block(totals, block_index):
        first_row = (block_index * ROWS_VIS).astype(jnp.int32)
        x_block = lax.dynamic_slice_in_dim(features, first_row, ROWS_VIS, 0).astype(jnp.float32)
        g_block = lax.dynamic_slice_in_dim(grad_rows, first_row, ROWS_VIS, 0).astype(jnp.float32)
        block_sum = jnp.einsum('rmw,rd->mwd', x_block, g_block)
        rounded = lax.optimization_barrier(block_sum.astype(jnp.bfloat16))
        return (totals + rounded.astype(jnp.float32), None)
    init = jnp.zeros((MERGE, VIS_W, D), jnp.float32)
    summed, _ = lax.scan(add_block, init, jnp.arange(N_VIS, dtype=jnp.int32))
    return (feature_grad, summed.astype(jnp.bfloat16))
```

```python
import functools

import jax
import jax.numpy as jnp
from jax import lax
from jax.experimental import pallas as pl
from jax.experimental.pallas import tpu as pltpu
from jax.sharding import PartitionSpec as P

MESH = pl.DeviceIdType.MESH
F32 = jnp.float32
BF16 = jnp.bfloat16
EPS = 1e-06
LANES = 128
CAP = 2
HALVES = 2


def remote(src, dst, send_sem, recv_sem, device):
    return pltpu.make_async_remote_copy(
        src_ref=src,
        dst_ref=dst,
        send_sem=send_sem,
        recv_sem=recv_sem,
        device_id=device,
        device_id_type=MESH,
    )


def kernel(
    sizes,
    x_ref,
    w_ref,
    gain_ref,
    pos_ref,
    cot_ref,
    fg_ref,
    wg_ref,
    pick,
    cot_cols,
    a2a_out,
    a2a_in,
    term,
    term_in,
    vals,
    scaled,
    stat_tile,
    stat_out,
    stat_in,
    grads,
    xt_plain,
    xt,
    own_part,
    sib_out,
    sib_in,
    right_out,
    right_in,
    left_out,
    left_in,
    row_part,
    row_in,
    cross_out,
    cross_in,
    fg_all,
    a2a_send,
    a2a_recv,
    term_send,
    term_recv,
    stat_send,
    stat_recv,
    grad_send,
    grad_recv,
    sib_send,
    sib_recv,
    right_send,
    right_recv,
    left_send,
    left_recv,
    row_send,
    row_recv,
    cross_send,
    cross_recv,
    full_send,
    full_recv,
):
    n_vis, n_tp, n_dp = sizes
    n_x = n_tp // 2
    n_z = n_vis // 2
    blocks = n_vis * n_dp
    rows = x_ref.shape[0]
    width = x_ref.shape[1]
    cols = w_ref.shape[1]
    per_block = rows // n_dp
    groups = cols // LANES
    slots_dev = cot_ref.shape[0]
    tile = CAP * groups
    total_cols = cols * n_tp
    half = cols // HALVES
    chunk = width // n_vis
    part_rows = rows // n_x
    part_cols = width // HALVES

    v = lax.axis_index("vis")
    t = lax.axis_index("tp")
    d = lax.axis_index("dp")
    z, core = v // 2, v % 2
    zh, xi = t // n_x, t % n_x
    me = v * n_dp + d

    def block_device(block):
        return {"vis": block // n_dp, "dp": block % n_dp}

    barrier = pltpu.get_barrier_semaphore()

    def greet(step, carry):
        pl.semaphore_signal(
            barrier, inc=1, device_id=block_device((me + step) % blocks), device_id_type=MESH
        )
        return carry

    for step in range(1, n_tp):
        pl.semaphore_signal(
            barrier, inc=1, device_id={"tp": (t + step) % n_tp}, device_id_type=MESH
        )
    lax.fori_loop(1, blocks, greet, 0)

    here = lax.broadcasted_iota(jnp.int32, (slots_dev, LANES), 0) + me * slots_dev
    block_at = jnp.full((slots_dev, LANES), -1, jnp.int32)
    for block in range(blocks):
        block_at = jnp.where(pos_ref[block : block + 1, :] == here, block, block_at)
    block_sub = jnp.broadcast_to(
        jnp.max(block_at.astype(F32), axis=1, keepdims=True), (slots_dev, LANES)
    )
    block_lane = block_sub.T
    first = lax.broadcasted_iota(jnp.int32, (LANES, LANES), 0)
    second = lax.broadcasted_iota(jnp.int32, (LANES, LANES), 1)
    earlier = jnp.where((block_sub == block_lane) & (first < second), 1.0, 0.0)
    rank = jnp.sum(earlier, axis=0, keepdims=True)
    slot = jnp.where(block_lane[0:1, :] < 0.0, -8192.0, block_lane[0:1, :] * CAP + rank)
    slot_row = slot.astype(jnp.int32) * groups
    out_row = lax.broadcasted_iota(jnp.int32, (blocks * tile, LANES), 0)
    for group in range(groups):
        span = pl.ds(group * LANES, LANES)
        pick[:, span] = jnp.where(out_row == slot_row + group, 1.0, 0.0).astype(BF16)
        cot_cols[pl.ds(group * slots_dev, slots_dev), :] = cot_ref[:, span]
    picked = jnp.dot(pick[...], cot_cols[...], preferred_element_type=F32).astype(BF16)
    a2a_out[...] = picked.reshape(blocks, tile, LANES)
    a2a_in[pl.ds(me, 1)] = a2a_out[pl.ds(me, 1)]

    pl.semaphore_wait(barrier, blocks - 1 + n_tp - 1)

    def send_slots(step, carry):
        block = (me + step) % blocks
        remote(
            a2a_out.at[block], a2a_in.at[me], a2a_send, a2a_recv, block_device(block)
        ).start()
        return carry

    lax.fori_loop(1, blocks, send_slots, 0)
    others = pl.ds(0, blocks - 1)
    a2a_all = remote(
        a2a_out.at[others], a2a_in.at[others], a2a_send, a2a_recv, block_device((me + 1) % blocks)
    )
    finish = [a2a_all.wait_send]

    order = [s for s in range(1, n_dp)]
    order.sort(key=lambda s: -min(s, n_dp - s))
    term_copies = []
    for h in range(HALVES):
        span = pl.ds(h * half, half)
        term[:, span] = jnp.dot(
            x_ref[...], w_ref[:, span], preferred_element_type=F32
        ).astype(BF16)
        for step in order:
            to = (d + step) % n_dp
            copy = remote(
                term.at[pl.ds(pl.multiple_of(to * per_block, 16), per_block), span],
                term_in.at[step - 1, :, span],
                term_send.at[h, step - 1],
                term_recv.at[h, step - 1],
                {"dp": to},
            )
            copy.start()
            term_copies.append(copy)
            finish.append(copy.wait_send)

    for start in range(0, width, LANES):
        xt_plain[pl.ds(start, LANES), :] = x_ref[:, pl.ds(start, LANES)].T
    for at in range(n_vis):
        xt[at % 2, pl.ds((at // 2) * chunk, chunk), :] = xt_plain[pl.ds(at * chunk, chunk), :]

    pos_lane = jnp.broadcast_to(pos_ref[pl.ds(me, 1), :], (LANES, LANES)).astype(F32)
    owner_lane = jnp.broadcast_to(
        pos_ref[pl.ds(me, 1), :] // slots_dev, (LANES, LANES)
    ).astype(F32)
    pos_sub = pos_lane.T
    owner_sub = owner_lane.T
    before = jnp.where((owner_sub == owner_lane) & (pos_lane < pos_sub), 1.0, 0.0)
    row_slot = owner_sub[:, 0:1] * CAP + jnp.sum(before, axis=1, keepdims=True)
    row_at = (row_slot[0:per_block] * groups).astype(jnp.int32)
    in_row = lax.broadcasted_iota(jnp.int32, (per_block, blocks * tile), 1)

    a2a_all.wait_recv()
    arrived = a2a_in[...].reshape(blocks * tile, LANES)
    for group in range(groups):
        span = pl.ds(group * LANES, LANES)
        select = jnp.where(in_row == row_at + group, 1.0, 0.0).astype(BF16)
        scaled[:, span] = (
            jnp.dot(select, arrived, preferred_element_type=F32) * gain_ref[:, span]
        )

    for copy in term_copies:
        copy.wait_recv()
    mine = pl.ds(pl.multiple_of(d * per_block, 16), per_block)
    total = term[mine, :].astype(F32)
    for step in range(1, n_dp):
        total = total + term_in[step - 1].astype(F32)
    value = total.astype(BF16).astype(F32)
    vals[...] = value
    square = jnp.sum(value * value, axis=1, keepdims=True)
    dotted = jnp.sum(scaled[...] * value, axis=1, keepdims=True)

    lane = lax.broadcasted_iota(jnp.int32, (per_block, LANES), 1)
    stat_tile[...] = jnp.zeros_like(stat_tile)
    stat_tile[0:per_block, :] = jnp.where(lane == 0, square, jnp.where(lane == 1, dotted, 0.0))
    stat_out[...] = stat_tile[...].T[0:8, :]
    stat_in[pl.ds(t, 1)] = stat_out[...].reshape(1, 8, LANES)
    stat_copies = []
    for step in sorted(range(1, n_tp), key=lambda s: -(s == n_x)):
        copy = remote(
            stat_out,
            stat_in.at[t],
            stat_send.at[step - 1],
            stat_recv.at[step - 1],
            {"tp": (t + step) % n_tp},
        )
        copy.start()
        stat_copies.append(copy)
        finish.append(copy.wait_send)
    for copy in stat_copies:
        copy.wait_recv()
    sums = stat_in[0]
    for at in range(1, n_tp):
        sums = sums + stat_in[at]
    inverse = lax.rsqrt(sums[0:1, :] / total_cols + EPS)
    factor = inverse * inverse * inverse * (sums[1:2, :] / total_cols)
    sub = lax.broadcasted_iota(jnp.int32, (LANES, LANES), 0)
    spread = jnp.where(sub == 0, inverse, jnp.where(sub == 1, factor, 0.0)).T
    inverse_col = spread[0:per_block, 0:1]
    factor_col = spread[0:per_block, 1:2]

    grad_copies = []
    for h in range(HALVES):
        span = pl.ds(h * half, half)
        grads[mine, span] = (
            inverse_col * scaled[:, span] - factor_col * vals[:, span]
        ).astype(BF16)
        copies = []
        for step in order:
            copy = remote(
                grads.at[mine, span],
                grads.at[mine, span],
                grad_send.at[h, step - 1],
                grad_recv.at[h, step - 1],
                {"dp": (d + step) % n_dp},
            )
            copy.start()
            finish.append(copy.wait_send)
            source = (d + n_dp - step) % n_dp
            landed = grads.at[
                pl.ds(pl.multiple_of(source * per_block, 16), per_block), span
            ]
            copies.append(
                remote(
                    landed,
                    landed,
                    grad_send.at[h, step - 1],
                    grad_recv.at[h, step - 1],
                    {"dp": (d + step) % n_dp},
                )
            )
        grad_copies.append(copies)

    sib_copies = []
    for h in range(HALVES):
        span = pl.ds(h * half, half)
        for copy in grad_copies[h]:
            copy.wait_recv()
        sib_out[h] = jnp.dot(
            xt[1 - core], grads[:, span], preferred_element_type=F32
        ).astype(BF16)
        copy = remote(
            sib_out.at[h],
            sib_in.at[h],
            sib_send.at[h],
            sib_recv.at[h],
            {"vis": v + 1 - 2 * core},
        )
        copy.start()
        sib_copies.append(copy)
        finish.append(copy.wait_send)
        own_part[h] = jnp.dot(xt[core], grads[:, span], preferred_element_type=F32).astype(BF16)

    x_order = sorted(range(1, n_x), key=lambda s: -min(s, n_x - s))

    def feature_products(f):
        span = pl.ds(f * part_cols, part_cols)
        row_part[:, span] = lax.dot_general(
            grads[...], w_ref[span, :], (((1,), (1,)), ((), ())), preferred_element_type=F32
        ).astype(BF16)
        copies = []
        for step in x_order:
            to = (xi + step) % n_x
            copy = remote(
                row_part.at[pl.ds(pl.multiple_of(to * part_rows, 16), part_rows), span],
                row_in.at[step - 1, :, span],
                row_send.at[f, step - 1],
                row_recv.at[f, step - 1],
                {"tp": zh * n_x + to},
            )
            copy.start()
            copies.append(copy)
            finish.append(copy.wait_send)
        return copies

    part = pl.ds(pl.multiple_of(xi * part_rows, 16), part_rows)

    def feature_cross(f, copies):
        span = pl.ds(f * part_cols, part_cols)
        for copy in copies:
            copy.wait_recv()
        summed = row_part[part, span].astype(F32)
        for step in range(1, n_x):
            summed = summed + row_in[step - 1, :, span].astype(F32)
        cross_out[f] = summed.astype(BF16)
        copy = remote(
            cross_out.at[f],
            cross_in.at[f],
            cross_send.at[f],
            cross_recv.at[f],
            {"tp": (t + n_x) % n_tp},
        )
        copy.start()
        finish.append(copy.wait_send)
        return copy

    def feature_spread(f, copy):
        span = pl.ds(f * part_cols, part_cols)
        copy.wait_recv()
        fg_all[part, span] = (cross_out[f].astype(F32) + cross_in[f].astype(F32)).astype(BF16)
        copies = []
        for step in x_order:
            send = remote(
                fg_all.at[part, span],
                fg_all.at[part, span],
                full_send.at[f, step - 1],
                full_recv.at[f, step - 1],
                {"tp": zh * n_x + (xi + step) % n_x},
            )
            send.start()
            finish.append(send.wait_send)
            source = (xi + n_x - step) % n_x
            landed = fg_all.at[
                pl.ds(pl.multiple_of(source * part_rows, 16), part_rows), span
            ]
            copies.append(
                remote(
                    landed,
                    landed,
                    full_send.at[f, step - 1],
                    full_recv.at[f, step - 1],
                    {"tp": zh * n_x + (xi + step) % n_x},
                )
            )
        return copies

    def line_copy(out, into, send_sem, recv_sem, at, h, to):
        return remote(
            out.at[at, h], into.at[at, h], send_sem.at[at, h], recv_sem.at[at, h], {"vis": to}
        )

    right = jnp.minimum(v + 2, n_vis - 2 + core)
    left = jnp.maximum(v - 2, core)

    def pair_sum(at, h):
        span = pl.ds(pl.multiple_of(at * chunk, 16), chunk)
        return own_part[h, span, :].astype(F32) + sib_in[h, span, :].astype(F32)

    def line_step(tau):
        for h in range(HALVES):

            @pl.when((z <= tau) & (z < n_z - 1) & (tau < n_z - 1))
            def _():
                at = n_z - 1 - tau + z
                copy = line_copy(right_out, right_in, right_send, right_recv, at, h, right)

                @pl.when(z > 0)
                def _():
                    copy.wait_recv()
                    right_out[at, h] = (
                        pair_sum(at, h) + right_in[at, h].astype(F32)
                    ).astype(BF16)

                @pl.when(z == 0)
                def _():
                    right_out[at, h] = pair_sum(at, h).astype(BF16)

                copy.start()

            @pl.when((n_z - 1 - z <= tau) & (z > 0) & (tau < n_z - 1))
            def _():
                at = tau - (n_z - 1 - z)
                copy = line_copy(left_out, left_in, left_send, left_recv, at, h, left)

                @pl.when(z < n_z - 1)
                def _():
                    copy.wait_recv()
                    left_out[at, h] = (
                        pair_sum(at, h) + left_in[at, h].astype(F32)
                    ).astype(BF16)

                @pl.when(z == n_z - 1)
                def _():
                    left_out[at, h] = pair_sum(at, h).astype(BF16)

                copy.start()

    def line_last():
        for h in range(HALVES):
            span = pl.ds(h * half, half)
            from_left = line_copy(right_out, right_in, right_send, right_recv, z, h, right)
            from_right = line_copy(left_out, left_in, left_send, left_recv, z, h, left)

            @pl.when(z > 0)
            def _():
                from_left.wait_recv()

            @pl.when(z < n_z - 1)
            def _():
                from_right.wait_recv()

            @pl.when(z == 0)
            def _():
                wg_ref[:, span] = (pair_sum(z, h) + left_in[z, h].astype(F32)).astype(BF16)

            @pl.when(z == n_z - 1)
            def _():
                wg_ref[:, span] = (pair_sum(z, h) + right_in[z, h].astype(F32)).astype(BF16)

            @pl.when((z > 0) & (z < n_z - 1))
            def _():
                wg_ref[:, span] = (
                    pair_sum(z, h) + right_in[z, h].astype(F32) + left_in[z, h].astype(F32)
                ).astype(BF16)

    def line_sent():
        for h in range(HALVES):

            def right_done(at, carry):
                line_copy(right_out, right_in, right_send, right_recv, at, h, right).wait_send()
                return carry

            def left_done(at, carry):
                line_copy(left_out, left_in, left_send, left_recv, at, h, left).wait_send()
                return carry

            lax.fori_loop(z + 1, n_z, right_done, 0)
            lax.fori_loop(0, z, left_done, 0)

    row_copies = [feature_products(f) for f in range(HALVES)]
    for copy in sib_copies:
        copy.wait_recv()
    line_step(0)
    line_step(1)
    cross = [feature_cross(0, row_copies[0])]
    line_step(2)
    cross.append(feature_cross(1, row_copies[1]))
    for tau in range(3, n_z - 2):
        line_step(tau)
    spread_copies = feature_spread(0, cross[0])
    for tau in range(max(3, n_z - 2), n_z - 1):
        line_step(tau)
    spread_copies += feature_spread(1, cross[1])
    line_last()
    for copy in spread_copies:
        copy.wait_recv()
    fg_ref[...] = fg_all[...]
    line_sent()
    for wait in finish:
        wait()


def on_device(features, merge_weight, gain, positions, cotangent):
    rows, sub_count, width = features.shape
    cols = merge_weight.shape[2]
    n_vis, n_tp, n_dp = (lax.axis_size(name) for name in ("vis", "tp", "dp"))
    blocks = n_vis * n_dp
    per_block = rows // n_dp
    slots_dev = cotangent.shape[0]
    groups = cols // LANES
    tile = CAP * groups
    n_x, n_z = n_tp // 2, n_vis // 2
    half = cols // HALVES
    chunk = width // n_vis
    share = width // 2
    part_rows = rows // n_x
    part_cols = width // HALVES
    table = jnp.pad(
        positions.reshape(blocks, per_block), ((0, 0), (0, LANES - per_block)), constant_values=-1
    )
    vmem = pl.BlockSpec(memory_space=pltpu.VMEM)
    dma = pltpu.SemaphoreType.DMA
    feature_grad, weight_grad = pl.pallas_call(
        functools.partial(kernel, (n_vis, n_tp, n_dp)),
        out_shape=(
            jax.ShapeDtypeStruct((rows, width), BF16),
            jax.ShapeDtypeStruct((chunk, cols), BF16),
        ),
        in_specs=[vmem] * 5,
        out_specs=(vmem, vmem),
        scratch_shapes=[
            pltpu.VMEM((blocks * tile, groups * slots_dev), BF16),
            pltpu.VMEM((groups * slots_dev, LANES), BF16),
            pltpu.VMEM((blocks, tile, LANES), BF16),
            pltpu.VMEM((blocks, tile, LANES), BF16),
            pltpu.VMEM((rows, cols), BF16),
            pltpu.VMEM((n_dp - 1, per_block, cols), BF16),
            pltpu.VMEM((per_block, cols), F32),
            pltpu.VMEM((per_block, cols), F32),
            pltpu.VMEM((LANES, LANES), F32),
            pltpu.VMEM((8, LANES), F32),
            pltpu.VMEM((n_tp, 8, LANES), F32),
            pltpu.VMEM((rows, cols), BF16),
            pltpu.VMEM((width, rows), BF16),
            pltpu.VMEM((2, share, rows), BF16),
            pltpu.VMEM((HALVES, share, half), BF16),
            pltpu.VMEM((HALVES, share, half), BF16),
            pltpu.VMEM((HALVES, share, half), BF16),
            pltpu.VMEM((n_z, HALVES, chunk, half), BF16),
            pltpu.VMEM((n_z, HALVES, chunk, half), BF16),
            pltpu.VMEM((n_z, HALVES, chunk, half), BF16),
            pltpu.VMEM((n_z, HALVES, chunk, half), BF16),
            pltpu.VMEM((rows, width), BF16),
            pltpu.VMEM((n_x - 1, part_rows, width), BF16),
            pltpu.VMEM((HALVES, part_rows, part_cols), BF16),
            pltpu.VMEM((HALVES, part_rows, part_cols), BF16),
            pltpu.VMEM((rows, width), BF16),
            dma,
            dma,
            dma((HALVES, n_dp - 1)),
            dma((HALVES, n_dp - 1)),
            dma((n_tp - 1,)),
            dma((n_tp - 1,)),
            dma((HALVES, n_dp - 1)),
            dma((HALVES, n_dp - 1)),
            dma((HALVES,)),
            dma((HALVES,)),
            dma((n_z, HALVES)),
            dma((n_z, HALVES)),
            dma((n_z, HALVES)),
            dma((n_z, HALVES)),
            dma((HALVES, n_x - 1)),
            dma((HALVES, n_x - 1)),
            dma((HALVES,)),
            dma((HALVES,)),
            dma((HALVES, n_x - 1)),
            dma((HALVES, n_x - 1)),
        ],
        compiler_params=pltpu.CompilerParams(
            collective_id=0, has_side_effects=True, vmem_limit_bytes=56 << 20
        ),
        cost_estimate=pl.CostEstimate(
            flops=6 * rows * width * cols, bytes_accessed=6 * width * cols, transcendentals=LANES
        ),
    )(
        features.reshape(rows, width),
        merge_weight.reshape(width, cols),
        gain.reshape(1, cols),
        table,
        cotangent,
    )
    return (feature_grad.reshape(features.shape), weight_grad.reshape(1, chunk, cols))


def solution(mesh):
    return jax.shard_map(
        on_device,
        mesh=mesh,
        in_specs=(P("vis", "dp", None), P("dp", None, "tp"), P("tp"), P(), P(("vis", "dp"), "tp")),
        out_specs=(P("vis", "dp", None), P("dp", "vis", "tp")),
        check_vma=False,
    )
```

```python
import functools

import jax
import jax.numpy as jnp
from jax import lax
from jax.experimental import pallas as pl
from jax.experimental.pallas import tpu as pltpu
from jax.sharding import PartitionSpec as P

MESH = pl.DeviceIdType.MESH
F32 = jnp.float32
BF16 = jnp.bfloat16
EPS = 1e-06
LANES = 128
CAP = 2
HALVES = 2
GROUPS = ((0, 16), (16, 16), (32, 32), (64, 32))
PIECES = 4
N_GROUPS = len(GROUPS)


def remote(src, dst, send_sem, recv_sem, device):
    return pltpu.make_async_remote_copy(
        src_ref=src,
        dst_ref=dst,
        send_sem=send_sem,
        recv_sem=recv_sem,
        device_id=device,
        device_id_type=MESH,
    )


def kernel(
    sizes,
    x_ref,
    w_ref,
    gain_ref,
    pos_ref,
    cot_ref,
    fg_ref,
    wg_ref,
    pick,
    cot_cols,
    a2a_out,
    a2a_in,
    term,
    term_in,
    vals,
    scaled,
    stat_tile,
    stat_out,
    stat_in,
    grads,
    xt_plain,
    xt,
    wt,
    own_part,
    sib_out,
    sib_in,
    right_out,
    right_in,
    left_out,
    left_in,
    row_part,
    row_in,
    cross_out,
    cross_in,
    fg_all,
    a2a_send,
    a2a_recv,
    term_send,
    term_recv,
    stat_send,
    stat_recv,
    grad_send,
    grad_recv,
    sib_send,
    sib_recv,
    right_send,
    right_recv,
    left_send,
    left_recv,
    row_send,
    row_recv,
    cross_send,
    cross_recv,
    full_send,
    full_recv,
):
    n_vis, n_tp, n_dp = sizes
    n_x = n_tp // 2
    n_z = n_vis // 2
    blocks = n_vis * n_dp
    rows = x_ref.shape[0]
    width = x_ref.shape[1]
    cols = w_ref.shape[1]
    per_block = rows // n_dp
    groups = cols // LANES
    slots_dev = cot_ref.shape[0]
    tile = CAP * groups
    total_cols = cols * n_tp
    half = cols // HALVES
    chunk = width // n_vis

    v = lax.axis_index("vis")
    t = lax.axis_index("tp")
    d = lax.axis_index("dp")
    z, core = v // 2, v % 2
    zh, xi = t // n_x, t % n_x
    me = v * n_dp + d

    def block_device(block):
        return {"vis": block // n_dp, "dp": block % n_dp}

    barrier = pltpu.get_barrier_semaphore()

    def greet(step, carry):
        pl.semaphore_signal(
            barrier, inc=1, device_id=block_device((me + step) % blocks), device_id_type=MESH
        )
        return carry

    for step in range(1, n_tp):
        pl.semaphore_signal(
            barrier, inc=1, device_id={"tp": (t + step) % n_tp}, device_id_type=MESH
        )
    lax.fori_loop(1, blocks, greet, 0)

    here = lax.broadcasted_iota(jnp.int32, (slots_dev, LANES), 0) + me * slots_dev
    block_at = jnp.full((slots_dev, LANES), -1, jnp.int32)
    for line in range(pos_ref.shape[0]):
        block_at = jnp.where(pos_ref[line : line + 1, :] == here, line, block_at)
    lane_at = lax.broadcasted_iota(jnp.int32, (slots_dev, LANES), 1)
    block_at = jnp.where(block_at < 0, -1, (block_at * LANES + lane_at) // per_block)
    block_sub = jnp.broadcast_to(
        jnp.max(block_at.astype(F32), axis=1, keepdims=True), (slots_dev, LANES)
    )
    block_lane = block_sub.T
    first = lax.broadcasted_iota(jnp.int32, (LANES, LANES), 0)
    second = lax.broadcasted_iota(jnp.int32, (LANES, LANES), 1)
    earlier = jnp.where((block_sub == block_lane) & (first < second), 1.0, 0.0)
    rank = jnp.sum(earlier, axis=0, keepdims=True)
    slot = jnp.where(block_lane[0:1, :] < 0.0, -8192.0, block_lane[0:1, :] * CAP + rank)
    slot_row = slot.astype(jnp.int32) * groups
    out_row = lax.broadcasted_iota(jnp.int32, (blocks * tile, LANES), 0)
    for group in range(groups):
        span = pl.ds(group * LANES, LANES)
        pick[:, span] = jnp.where(out_row == slot_row + group, 1.0, 0.0).astype(BF16)
        cot_cols[pl.ds(group * slots_dev, slots_dev), :] = cot_ref[:, span]
    picked = jnp.dot(pick[...], cot_cols[...], preferred_element_type=F32).astype(BF16)
    a2a_out[...] = picked.reshape(blocks, tile, LANES)
    a2a_in[pl.ds(me, 1)] = a2a_out[pl.ds(me, 1)]

    pl.semaphore_wait(barrier, blocks - 1 + n_tp - 1)

    def send_slots(step, carry):
        block = (me + step) % blocks
        remote(
            a2a_out.at[block], a2a_in.at[me], a2a_send, a2a_recv, block_device(block)
        ).start()
        return carry

    lax.fori_loop(1, blocks, send_slots, 0)
    others = pl.ds(0, blocks - 1)
    a2a_all = remote(
        a2a_out.at[others], a2a_in.at[others], a2a_send, a2a_recv, block_device((me + 1) % blocks)
    )
    finish = [a2a_all.wait_send]

    order = [s for s in range(1, n_dp)]
    order.sort(key=lambda s: -min(s, n_dp - s))
    term_copies = []
    for h in range(HALVES):
        span = pl.ds(h * half, half)
        term[:, span] = jnp.dot(
            x_ref[...], w_ref[:, span], preferred_element_type=F32
        ).astype(BF16)
        for step in order:
            to = (d + step) % n_dp
            copy = remote(
                term.at[pl.ds(pl.multiple_of(to * per_block, 16), per_block), span],
                term_in.at[step - 1, :, span],
                term_send.at[h, step - 1],
                term_recv.at[h, step - 1],
                {"dp": to},
            )
            copy.start()
            term_copies.append(copy)
            finish.append(copy.wait_send)

    for start in range(0, width, LANES):
        xt_plain[pl.ds(start, LANES), :] = x_ref[:, pl.ds(start, LANES)].T
    for at in range(n_vis):
        xt[at % 2, pl.ds((at // 2) * chunk, chunk), :] = xt_plain[pl.ds(at * chunk, chunk), :]

    for start in range(0, cols, LANES):
        wt[pl.ds(start, LANES), :] = w_ref[:, pl.ds(start, LANES)].T

    flat = lax.broadcasted_iota(jnp.int32, (LANES, LANES), 0) + me * per_block
    line_first = (me * per_block) // LANES
    line_next = jnp.minimum(line_first + 1, pos_ref.shape[0] - 1)
    line_pos = jnp.where(
        flat // LANES == line_first, pos_ref[pl.ds(line_first, 1), :], pos_ref[pl.ds(line_next, 1), :]
    )
    row_pos = jnp.sum(
        jnp.where(flat % LANES == second, line_pos, 0).astype(F32), axis=1, keepdims=True
    )
    row_pos = jnp.where(first[:, 0:1] < per_block, row_pos, -1.0)
    pos_sub = jnp.broadcast_to(row_pos, (LANES, LANES))
    owner_sub = jnp.floor(pos_sub / slots_dev)
    pos_lane = pos_sub.T
    owner_lane = owner_sub.T
    before = jnp.where((owner_sub == owner_lane) & (pos_lane < pos_sub), 1.0, 0.0)
    row_slot = owner_sub[:, 0:1] * CAP + jnp.sum(before, axis=1, keepdims=True)
    row_at = (row_slot[0:per_block] * groups).astype(jnp.int32)
    in_row = lax.broadcasted_iota(jnp.int32, (per_block, blocks * tile), 1)

    a2a_all.wait_recv()
    arrived = a2a_in[...].reshape(blocks * tile, LANES)
    for group in range(groups):
        span = pl.ds(group * LANES, LANES)
        select = jnp.where(in_row == row_at + group, 1.0, 0.0).astype(BF16)
        scaled[:, span] = (
            jnp.dot(select, arrived, preferred_element_type=F32) * gain_ref[:, span]
        )

    for copy in term_copies:
        copy.wait_recv()
    mine = pl.ds(pl.multiple_of(d * per_block, 16), per_block)
    total = term[mine, :].astype(F32)
    for step in range(1, n_dp):
        total = total + term_in[step - 1].astype(F32)
    value = total.astype(BF16).astype(F32)
    vals[...] = value
    square = jnp.sum(value * value, axis=1, keepdims=True)
    dotted = jnp.sum(scaled[...] * value, axis=1, keepdims=True)

    lane = lax.broadcasted_iota(jnp.int32, (per_block, LANES), 1)
    stat_tile[...] = jnp.zeros_like(stat_tile)
    stat_tile[0:per_block, :] = jnp.where(lane == 0, square, jnp.where(lane == 1, dotted, 0.0))
    stat_out[...] = stat_tile[...].T[0:8, :]
    stat_in[pl.ds(t, 1)] = stat_out[...].reshape(1, 8, LANES)
    stat_copies = []
    for step in sorted(range(1, n_tp), key=lambda s: -(s == n_x)):
        copy = remote(
            stat_out,
            stat_in.at[t],
            stat_send.at[step - 1],
            stat_recv.at[step - 1],
            {"tp": (t + step) % n_tp},
        )
        copy.start()
        stat_copies.append(copy)
        finish.append(copy.wait_send)
    for copy in stat_copies:
        copy.wait_recv()
    sums = stat_in[0]
    for at in range(1, n_tp):
        sums = sums + stat_in[at]
    inverse = lax.rsqrt(sums[0:1, :] / total_cols + EPS)
    factor = inverse * inverse * inverse * (sums[1:2, :] / total_cols)
    sub = lax.broadcasted_iota(jnp.int32, (LANES, LANES), 0)
    spread = jnp.where(sub == 0, inverse, jnp.where(sub == 1, factor, 0.0)).T
    inverse_col = spread[0:per_block, 0:1]
    factor_col = spread[0:per_block, 1:2]

    grad_copies = []
    grad_sent = []

    def send_grads(g):
        at, size = GROUPS[g]
        inside = pl.ds(at, size)
        group = pl.ds(pl.multiple_of(d * per_block + at, 16), size)
        grads[group, :] = (
            inverse_col[at : at + size] * scaled[inside, :]
            - factor_col[at : at + size] * vals[inside, :]
        ).astype(BF16)
        arrivals, sent = [], []
        for step in order:
            to = {"dp": (d + step) % n_dp}
            sems = grad_send.at[g, step - 1], grad_recv.at[g, step - 1]
            copy = remote(grads.at[group], grads.at[group], *sems, to)
            copy.start()
            sent.append(copy.wait_send)
            source = (d + n_dp - step) % n_dp
            landed = grads.at[pl.ds(pl.multiple_of(source * per_block + at, 16), size)]
            arrivals.append(remote(landed, landed, *sems, to))
        grad_copies.append(arrivals)
        grad_sent.append(sent)

    def grads_gone(g):
        for wait in grad_sent[g]:
            wait()

    sib_copies = []

    def share_out(h):
        span = pl.ds(h * half, half)
        sib_out[h] = jnp.dot(
            xt[1 - core], grads[:, span], preferred_element_type=F32
        ).astype(BF16)
        copy = remote(
            sib_out.at[h],
            sib_in.at[h],
            sib_send.at[h],
            sib_recv.at[h],
            {"vis": v + 1 - 2 * core},
        )
        copy.start()
        sib_copies.append(copy)
        finish.append(copy.wait_send)

    def share_own(h):
        span = pl.ds(h * half, half)
        own_part[h] = jnp.dot(xt[core], grads[:, span], preferred_element_type=F32).astype(BF16)

    x_order = sorted(range(1, n_x), key=lambda s: -min(s, n_x - s))

    def feature_products(g):
        at, size = GROUPS[g]
        for copy in grad_copies[g]:
            copy.wait_recv()
        group = jnp.concatenate(
            [grads[pl.ds(block * per_block + at, size), :] for block in range(n_dp)], axis=0
        )
        row_part[pl.ds(n_dp * at, n_dp * size), :] = jnp.dot(
            group, wt[...], preferred_element_type=F32
        ).astype(BF16)
        copies = []
        for step in x_order:
            to = (xi + step) % n_x
            copy = remote(
                row_part.at[pl.ds(pl.multiple_of(n_dp * at + to * size, 16), size)],
                row_in.at[step - 1, pl.ds(at, size)],
                row_send.at[g, step - 1],
                row_recv.at[g, step - 1],
                {"tp": zh * n_x + to},
            )
            copy.start()
            copies.append(copy)
            finish.append(copy.wait_send)
        return copies

    def feature_cross(g, copies):
        at, size = GROUPS[g]
        inside = pl.ds(at, size)
        for copy in copies:
            copy.wait_recv()
        summed = row_part[
            pl.ds(pl.multiple_of(n_dp * at + xi * size, 16), size), :
        ].astype(F32)
        for step in range(1, n_x):
            summed = summed + row_in[step - 1, inside, :].astype(F32)
        cross_out[inside, :] = summed.astype(BF16)
        copy = remote(
            cross_out.at[inside],
            cross_in.at[inside],
            cross_send.at[g],
            cross_recv.at[g],
            {"tp": (t + n_x) % n_tp},
        )
        copy.start()
        finish.append(copy.wait_send)
        return copy

    def feature_spread(g, copy):
        at, size = GROUPS[g]
        inside = pl.ds(at, size)
        copy.wait_recv()
        place = pl.ds(pl.multiple_of(xi * per_block + at, 16), size)
        fg_all[place, :] = (
            cross_out[inside, :].astype(F32) + cross_in[inside, :].astype(F32)
        ).astype(BF16)
        copies = []
        for step in x_order:
            to = {"tp": zh * n_x + (xi + step) % n_x}
            sems = full_send.at[g, step - 1], full_recv.at[g, step - 1]
            send = remote(fg_all.at[place], fg_all.at[place], *sems, to)
            send.start()
            finish.append(send.wait_send)
            source = (xi + n_x - step) % n_x
            landed = fg_all.at[pl.ds(pl.multiple_of(source * per_block + at, 16), size)]
            copies.append(remote(landed, landed, *sems, to))
        return copies

    def line_copy(out, into, send_sem, recv_sem, at, h, to):
        return remote(
            out.at[at, h], into.at[at, h], send_sem.at[at, h], recv_sem.at[at, h], {"vis": to}
        )

    right = jnp.minimum(v + 2, n_vis - 2 + core)
    left = jnp.maximum(v - 2, core)

    def pair_sum(at, h):
        span = pl.ds(pl.multiple_of(at * chunk, 16), chunk)
        return own_part[h, span, :].astype(F32) + sib_in[h, span, :].astype(F32)

    def line_step(tau):
        for h in range(HALVES):

            @pl.when((z <= tau) & (z < n_z - 1) & (tau < n_z - 1))
            def _():
                at = n_z - 1 - tau + z
                copy = line_copy(right_out, right_in, right_send, right_recv, at, h, right)

                @pl.when(z > 0)
                def _():
                    copy.wait_recv()
                    right_out[at, h] = (
                        pair_sum(at, h) + right_in[at, h].astype(F32)
                    ).astype(BF16)

                @pl.when(z == 0)
                def _():
                    right_out[at, h] = pair_sum(at, h).astype(BF16)

                copy.start()

            @pl.when((n_z - 1 - z <= tau) & (z > 0) & (tau < n_z - 1))
            def _():
                at = tau - (n_z - 1 - z)
                copy = line_copy(left_out, left_in, left_send, left_recv, at, h, left)

                @pl.when(z < n_z - 1)
                def _():
                    copy.wait_recv()
                    left_out[at, h] = (
                        pair_sum(at, h) + left_in[at, h].astype(F32)
                    ).astype(BF16)

                @pl.when(z == n_z - 1)
                def _():
                    left_out[at, h] = pair_sum(at, h).astype(BF16)

                copy.start()

    def line_last():
        for h in range(HALVES):
            span = pl.ds(h * half, half)
            from_left = line_copy(right_out, right_in, right_send, right_recv, z, h, right)
            from_right = line_copy(left_out, left_in, left_send, left_recv, z, h, left)

            @pl.when(z > 0)
            def _():
                from_left.wait_recv()

            @pl.when(z < n_z - 1)
            def _():
                from_right.wait_recv()

            @pl.when(z == 0)
            def _():
                wg_ref[:, span] = (pair_sum(z, h) + left_in[z, h].astype(F32)).astype(BF16)

            @pl.when(z == n_z - 1)
            def _():
                wg_ref[:, span] = (pair_sum(z, h) + right_in[z, h].astype(F32)).astype(BF16)

            @pl.when((z > 0) & (z < n_z - 1))
            def _():
                wg_ref[:, span] = (
                    pair_sum(z, h) + right_in[z, h].astype(F32) + left_in[z, h].astype(F32)
                ).astype(BF16)

    def line_sent():
        for h in range(HALVES):

            def right_done(at, carry):
                line_copy(right_out, right_in, right_send, right_recv, at, h, right).wait_send()
                return carry

            def left_done(at, carry):
                line_copy(left_out, left_in, left_send, left_recv, at, h, left).wait_send()
                return carry

            lax.fori_loop(z + 1, n_z, right_done, 0)
            lax.fori_loop(0, z, left_done, 0)

    send_grads(0)
    send_grads(1)
    row_copies = [feature_products(0)]
    grads_gone(0)
    send_grads(2)
    row_copies.append(feature_products(1))
    grads_gone(1)
    send_grads(3)
    cross = [feature_cross(0, row_copies[0])]
    row_copies.append(feature_products(2))
    cross.append(feature_cross(1, row_copies[1]))
    row_copies.append(feature_products(3))
    share_out(0)
    share_out(1)
    cross.append(feature_cross(2, row_copies[2]))
    share_own(0)
    share_own(1)
    for copy in sib_copies:
        copy.wait_recv()
    cross.append(feature_cross(3, row_copies[3]))
    spread_copies = feature_spread(0, cross[0])
    line_step(0)
    spread_copies += feature_spread(1, cross[1])
    line_step(1)
    line_step(2)
    spread_copies += feature_spread(2, cross[2])
    line_step(3)
    spread_copies += feature_spread(3, cross[3])
    line_step(4)
    line_step(5)
    line_step(6)
    line_last()
    for copy in spread_copies:
        copy.wait_recv()
    fg_ref[...] = fg_all[...]
    line_sent()
    grads_gone(2)
    grads_gone(3)
    for wait in finish:
        wait()


def hand_on(fg_in, wg_in, fg_ref, wg_ref, fg_held, wg_held, sems_in, sems_out):
    pieces = sems_in.shape[0] - 1
    size = fg_in.shape[0] // pieces
    spans = [pl.ds(at * size, size) for at in range(pieces)]
    sources = [fg_in.at[span] for span in spans] + [wg_in]
    held = [fg_held.at[span] for span in spans] + [wg_held]
    targets = [fg_ref.at[span] for span in spans] + [wg_ref]
    into = [pltpu.make_async_copy(a, b, sems_in.at[k]) for k, (a, b) in enumerate(zip(sources, held))]
    out = [pltpu.make_async_copy(a, b, sems_out.at[k]) for k, (a, b) in enumerate(zip(held, targets))]
    for copy in into:
        copy.start()
    for first, second in zip(into, out):
        first.wait()
        second.start()
    for copy in out:
        copy.wait()


def on_device(features, merge_weight, gain, positions, cotangent):
    rows, sub_count, width = features.shape
    cols = merge_weight.shape[2]
    n_vis, n_tp, n_dp = (lax.axis_size(name) for name in ("vis", "tp", "dp"))
    blocks = n_vis * n_dp
    per_block = rows // n_dp
    slots_dev = cotangent.shape[0]
    groups = cols // LANES
    tile = CAP * groups
    n_x, n_z = n_tp // 2, n_vis // 2
    half = cols // HALVES
    chunk = width // n_vis
    share = width // 2
    vmem = pl.BlockSpec(memory_space=pltpu.VMEM)
    dma = pltpu.SemaphoreType.DMA
    feature_grad, weight_grad = pl.pallas_call(
        functools.partial(kernel, (n_vis, n_tp, n_dp)),
        out_shape=(
            jax.ShapeDtypeStruct((rows, width), BF16),
            jax.ShapeDtypeStruct((chunk, cols), BF16),
        ),
        in_specs=[vmem] * 5,
        out_specs=(vmem, vmem),
        scratch_shapes=[
            pltpu.VMEM((blocks * tile, groups * slots_dev), BF16),
            pltpu.VMEM((groups * slots_dev, LANES), BF16),
            pltpu.VMEM((blocks, tile, LANES), BF16),
            pltpu.VMEM((blocks, tile, LANES), BF16),
            pltpu.VMEM((rows, cols), BF16),
            pltpu.VMEM((n_dp - 1, per_block, cols), BF16),
            pltpu.VMEM((per_block, cols), F32),
            pltpu.VMEM((per_block, cols), F32),
            pltpu.VMEM((LANES, LANES), F32),
            pltpu.VMEM((8, LANES), F32),
            pltpu.VMEM((n_tp, 8, LANES), F32),
            pltpu.VMEM((rows, cols), BF16),
            pltpu.VMEM((width, rows), BF16),
            pltpu.VMEM((2, share, rows), BF16),
            pltpu.VMEM((cols, width), BF16),
            pltpu.VMEM((HALVES, share, half), BF16),
            pltpu.VMEM((HALVES, share, half), BF16),
            pltpu.VMEM((HALVES, share, half), BF16),
            pltpu.VMEM((n_z, HALVES, chunk, half), BF16),
            pltpu.VMEM((n_z, HALVES, chunk, half), BF16),
            pltpu.VMEM((n_z, HALVES, chunk, half), BF16),
            pltpu.VMEM((n_z, HALVES, chunk, half), BF16),
            pltpu.VMEM((rows, width), BF16),
            pltpu.VMEM((n_x - 1, per_block, width), BF16),
            pltpu.VMEM((per_block, width), BF16),
            pltpu.VMEM((per_block, width), BF16),
            pltpu.VMEM((rows, width), BF16),
            dma,
            dma,
            dma((HALVES, n_dp - 1)),
            dma((HALVES, n_dp - 1)),
            dma((n_tp - 1,)),
            dma((n_tp - 1,)),
            dma((N_GROUPS, n_dp - 1)),
            dma((N_GROUPS, n_dp - 1)),
            dma((HALVES,)),
            dma((HALVES,)),
            dma((n_z, HALVES)),
            dma((n_z, HALVES)),
            dma((n_z, HALVES)),
            dma((n_z, HALVES)),
            dma((N_GROUPS, n_x - 1)),
            dma((N_GROUPS, n_x - 1)),
            dma((N_GROUPS,)),
            dma((N_GROUPS,)),
            dma((N_GROUPS, n_x - 1)),
            dma((N_GROUPS, n_x - 1)),
        ],
        compiler_params=pltpu.CompilerParams(
            collective_id=0, has_side_effects=True, vmem_limit_bytes=56 << 20
        ),
        cost_estimate=pl.CostEstimate(
            flops=6 * rows * width * cols, bytes_accessed=6 * width * cols, transcendentals=LANES
        ),
    )(
        features.reshape(rows, width),
        merge_weight.reshape(width, cols),
        gain.reshape(1, cols),
        positions.reshape(-1, LANES),
        cotangent,
    )
    anywhere = pl.BlockSpec(memory_space=pl.ANY)
    feature_grad, weight_grad = pl.pallas_call(
        hand_on,
        out_shape=(
            jax.ShapeDtypeStruct((rows, width), BF16),
            jax.ShapeDtypeStruct((chunk, cols), BF16),
        ),
        in_specs=[anywhere] * 2,
        out_specs=(anywhere, anywhere),
        scratch_shapes=[
            pltpu.VMEM((rows, width), BF16),
            pltpu.VMEM((chunk, cols), BF16),
            dma((PIECES + 1,)),
            dma((PIECES + 1,)),
        ],
        compiler_params=pltpu.CompilerParams(vmem_limit_bytes=60 << 20),
    )(feature_grad, weight_grad)
    return (feature_grad.reshape(features.shape), weight_grad.reshape(1, chunk, cols))


def solution(mesh):
    return jax.shard_map(
        on_device,
        mesh=mesh,
        in_specs=(P("vis", "dp", None), P("dp", None, "tp"), P("tp"), P(), P(("vis", "dp"), "tp")),
        out_specs=(P("vis", "dp", None), P("dp", "vis", "tp")),
        check_vma=False,
    )
```

```python
import functools

import jax
import jax.numpy as jnp
from jax import lax
from jax.experimental import pallas as pl
from jax.experimental.pallas import tpu as pltpu
from jax.sharding import PartitionSpec as P

MESH = pl.DeviceIdType.MESH
F32 = jnp.float32
BF16 = jnp.bfloat16
EPS = 1e-06
LANES = 128
CAP = 2
HALVES = 2
STRIP = 16
SENDS = 4
PIECES = 4


def remote(src, dst, send_sem, recv_sem, device):
    return pltpu.make_async_remote_copy(
        src_ref=src,
        dst_ref=dst,
        send_sem=send_sem,
        recv_sem=recv_sem,
        device_id=device,
        device_id_type=MESH,
    )


def kernel(
    sizes,
    x_ref,
    w_ref,
    gain_ref,
    pos_ref,
    cot_ref,
    fg_ref,
    wg_ref,
    slots_wide,
    a2a_out,
    a2a_in,
    term,
    term_in,
    vals,
    scaled,
    stat_tile,
    stat_out,
    stat_in,
    grads,
    xt_plain,
    xt,
    wt,
    own_part,
    sib_out,
    sib_in,
    right_out,
    right_in,
    left_out,
    left_in,
    row_part,
    row_in,
    cross_out,
    cross_in,
    fg_all,
    a2a_send,
    a2a_recv,
    term_send,
    term_recv,
    stat_send,
    stat_recv,
    grad_send,
    grad_recv,
    sib_send,
    sib_recv,
    right_send,
    right_recv,
    left_send,
    left_recv,
    row_send,
    row_recv,
    cross_send,
    cross_recv,
    full_send,
    full_recv,
):
    n_vis, n_tp, n_dp = sizes
    n_x = n_tp // 2
    n_z = n_vis // 2
    blocks = n_vis * n_dp
    rows = x_ref.shape[0]
    width = x_ref.shape[1]
    cols = w_ref.shape[1]
    per_block = rows // n_dp
    groups = cols // LANES
    slots_dev = cot_ref.shape[0]
    tile = CAP * groups
    total_cols = cols * n_tp
    half = cols // HALVES
    chunk = width // n_vis

    v = lax.axis_index("vis")
    t = lax.axis_index("tp")
    d = lax.axis_index("dp")
    z, core = v // 2, v % 2
    zh, xi = t // n_x, t % n_x
    me = v * n_dp + d

    def block_device(block):
        return {"vis": block // n_dp, "dp": block % n_dp}

    barrier = pltpu.get_barrier_semaphore()

    def greet(step, carry):
        pl.semaphore_signal(
            barrier, inc=1, device_id=block_device((me + step) % blocks), device_id_type=MESH
        )
        return carry

    for step in range(1, n_tp):
        pl.semaphore_signal(
            barrier, inc=1, device_id={"tp": (t + step) % n_tp}, device_id_type=MESH
        )
    lax.fori_loop(1, blocks, greet, 0)

    here = lax.broadcasted_iota(jnp.int32, (slots_dev, LANES), 0) + me * slots_dev
    block_at = jnp.full((slots_dev, LANES), -1, jnp.int32)
    for line in range(pos_ref.shape[0]):
        block_at = jnp.where(pos_ref[line : line + 1, :] == here, line, block_at)
    lane_at = lax.broadcasted_iota(jnp.int32, (slots_dev, LANES), 1)
    block_at = jnp.where(block_at < 0, -1, (block_at * LANES + lane_at) // per_block)
    block_sub = jnp.broadcast_to(
        jnp.max(block_at.astype(F32), axis=1, keepdims=True), (slots_dev, LANES)
    )
    block_lane = block_sub.T
    first = lax.broadcasted_iota(jnp.int32, (LANES, LANES), 0)
    second = lax.broadcasted_iota(jnp.int32, (LANES, LANES), 1)
    earlier = jnp.where((block_sub == block_lane) & (first < second), 1.0, 0.0)
    rank = jnp.sum(earlier, axis=0, keepdims=True)
    slot = jnp.where(block_lane[0:1, :] < 0.0, -8192.0, block_lane[0:1, :] * CAP + rank)
    slot_row = slot.astype(jnp.int32)
    pick = jnp.where(
        lax.broadcasted_iota(jnp.int32, (blocks * CAP, LANES), 0) == slot_row, 1.0, 0.0
    ).astype(BF16)
    for group in range(groups):
        slots_wide[pl.ds(group, blocks * CAP, stride=groups), :] = jnp.dot(
            pick, cot_ref[:, pl.ds(group * LANES, LANES)], preferred_element_type=F32
        )
    a2a_out[...] = slots_wide[...].astype(BF16).reshape(blocks, tile, LANES)
    a2a_in[pl.ds(me, 1)] = a2a_out[pl.ds(me, 1)]

    pl.semaphore_wait(barrier, blocks - 1 + n_tp - 1)

    def send_slots(step, carry):
        block = (me + step) % blocks
        remote(
            a2a_out.at[block], a2a_in.at[me], a2a_send, a2a_recv, block_device(block)
        ).start()
        return carry

    lax.fori_loop(1, blocks, send_slots, 0)
    others = pl.ds(0, blocks - 1)
    a2a_all = remote(
        a2a_out.at[others], a2a_in.at[others], a2a_send, a2a_recv, block_device((me + 1) % blocks)
    )
    finish = [a2a_all.wait_send]

    order = [s for s in range(1, n_dp)]
    order.sort(key=lambda s: -min(s, n_dp - s))
    term_copies = []
    for h in range(HALVES):
        span = pl.ds(h * half, half)
        term[:, span] = jnp.dot(
            x_ref[...], w_ref[:, span], preferred_element_type=F32
        ).astype(BF16)
        for step in order:
            to = (d + step) % n_dp
            copy = remote(
                term.at[pl.ds(pl.multiple_of(to * per_block, 16), per_block), span],
                term_in.at[step - 1, :, span],
                term_send.at[h, step - 1],
                term_recv.at[h, step - 1],
                {"dp": to},
            )
            copy.start()
            term_copies.append(copy)
            finish.append(copy.wait_send)

    for start in range(0, width, LANES):
        xt_plain[pl.ds(start, LANES), :] = x_ref[:, pl.ds(start, LANES)].T
    for at in range(n_vis):
        xt[at % 2, pl.ds((at // 2) * chunk, chunk), :] = xt_plain[pl.ds(at * chunk, chunk), :]

    for start in range(0, cols, LANES):
        wt[pl.ds(start, LANES), :] = w_ref[:, pl.ds(start, LANES)].T

    flat = lax.broadcasted_iota(jnp.int32, (LANES, LANES), 0) + me * per_block
    line_first = (me * per_block) // LANES
    line_next = jnp.minimum(line_first + 1, pos_ref.shape[0] - 1)
    line_pos = jnp.where(
        flat // LANES == line_first, pos_ref[pl.ds(line_first, 1), :], pos_ref[pl.ds(line_next, 1), :]
    )
    row_pos = jnp.sum(
        jnp.where(flat % LANES == second, line_pos, 0).astype(F32), axis=1, keepdims=True
    )
    row_pos = jnp.where(first[:, 0:1] < per_block, row_pos, -1.0)
    pos_sub = jnp.broadcast_to(row_pos, (LANES, LANES))
    owner_sub = jnp.floor(pos_sub / slots_dev)
    pos_lane = pos_sub.T
    owner_lane = owner_sub.T
    before = jnp.where((owner_sub == owner_lane) & (pos_lane < pos_sub), 1.0, 0.0)
    row_slot = owner_sub[:, 0:1] * CAP + jnp.sum(before, axis=1, keepdims=True)
    in_slot = lax.broadcasted_iota(jnp.int32, (per_block, blocks * CAP), 1)
    select = jnp.where(
        in_slot == row_slot[0:per_block].astype(jnp.int32), 1.0, 0.0
    ).astype(BF16)

    a2a_all.wait_recv()
    slots_wide[...] = a2a_in[...].reshape(blocks * tile, LANES).astype(F32)
    for group in range(groups):
        span = pl.ds(group * LANES, LANES)
        arrived = slots_wide[pl.ds(group, blocks * CAP, stride=groups), :].astype(BF16)
        scaled[:, span] = (
            jnp.dot(select, arrived, preferred_element_type=F32) * gain_ref[:, span]
        )

    for copy in term_copies:
        copy.wait_recv()
    mine = pl.ds(pl.multiple_of(d * per_block, 16), per_block)
    total = term[mine, :].astype(F32)
    for step in range(1, n_dp):
        total = total + term_in[step - 1].astype(F32)
    value = total.astype(BF16).astype(F32)
    vals[...] = value
    square = jnp.sum(value * value, axis=1, keepdims=True)
    dotted = jnp.sum(scaled[...] * value, axis=1, keepdims=True)

    lane = lax.broadcasted_iota(jnp.int32, (per_block, LANES), 1)
    stat_tile[...] = jnp.zeros_like(stat_tile)
    stat_tile[0:per_block, :] = jnp.where(lane == 0, square, jnp.where(lane == 1, dotted, 0.0))
    stat_out[...] = stat_tile[...].T[0:8, :]
    stat_in[pl.ds(t, 1)] = stat_out[...].reshape(1, 8, LANES)
    stat_copies = []
    for step in sorted(range(1, n_tp), key=lambda s: -(s == n_x)):
        copy = remote(
            stat_out,
            stat_in.at[t],
            stat_send.at[step - 1],
            stat_recv.at[step - 1],
            {"tp": (t + step) % n_tp},
        )
        copy.start()
        stat_copies.append(copy)
        finish.append(copy.wait_send)
    for copy in stat_copies:
        copy.wait_recv()
    sums = stat_in[0]
    for at in range(1, n_tp):
        sums = sums + stat_in[at]
    inverse = lax.rsqrt(sums[0:1, :] / total_cols + EPS)
    factor = inverse * inverse * inverse * (sums[1:2, :] / total_cols)
    sub = lax.broadcasted_iota(jnp.int32, (LANES, LANES), 0)
    spread = jnp.where(sub == 0, inverse, jnp.where(sub == 1, factor, 0.0)).T
    inverse_col = spread[0:per_block, 0:1]
    factor_col = spread[0:per_block, 1:2]

    rest = per_block - 2 * STRIP
    sends = (
        (0, STRIP, pl.ds(0, cols)),
        (STRIP, STRIP, pl.ds(0, cols)),
        (2 * STRIP, rest, pl.ds(0, half)),
        (2 * STRIP, rest, pl.ds(half, half)),
    )
    grads[mine, :] = (inverse_col * scaled[...] - factor_col * vals[...]).astype(BF16)
    grad_copies = []
    grad_sent = []

    def send_grads(g):
        at, size, span = sends[g]
        group = pl.ds(pl.multiple_of(d * per_block + at, 16), size)
        arrivals, sent = {}, []
        for step in order:
            to = {"dp": (d + step) % n_dp}
            sems = grad_send.at[g, step - 1], grad_recv.at[g, step - 1]
            copy = remote(grads.at[group, span], grads.at[group, span], *sems, to)
            copy.start()
            sent.append(copy.wait_send)
            source = (d + n_dp - step) % n_dp
            landed = grads.at[
                pl.ds(pl.multiple_of(source * per_block + at, 16), size), span
            ]
            arrivals[step] = remote(landed, landed, *sems, to)
        grad_copies.append(arrivals)
        grad_sent.append(sent)

    def grads_here(g):
        for copy in grad_copies[g].values():
            copy.wait_recv()

    def grads_gone(g):
        for wait in grad_sent[g]:
            wait()

    sib_copies = []

    def share_out(h):
        span = pl.ds(h * half, half)
        sib_out[h] = jnp.dot(
            xt[1 - core], grads[:, span], preferred_element_type=F32
        ).astype(BF16)
        copy = remote(
            sib_out.at[h],
            sib_in.at[h],
            sib_send.at[h],
            sib_recv.at[h],
            {"vis": v + 1 - 2 * core},
        )
        copy.start()
        sib_copies.append(copy)
        finish.append(copy.wait_send)

    def share_own(h):
        span = pl.ds(h * half, half)
        own_part[h] = jnp.dot(xt[core], grads[:, span], preferred_element_type=F32).astype(BF16)

    x_order = sorted(range(1, n_x), key=lambda s: -min(s, n_x - s))
    group_rows = STRIP * n_x

    def strip_row(g, at):
        if g == 0:
            row = d * per_block + at * STRIP
        elif g < 3:
            row = jnp.where(
                at == 0,
                d * per_block + group_rows + (g - 1) * STRIP,
                ((d + at) % n_dp) * per_block + (g - 1) * STRIP,
            )
        else:
            row = ((d + g - 2) % n_dp) * per_block + 2 * STRIP + at * STRIP
        return pl.ds(pl.multiple_of(row, 16), STRIP)

    def feature_products(g):
        group = jnp.concatenate([grads[strip_row(g, at), :] for at in range(n_x)], axis=0)
        row_part[pl.ds(g * group_rows, group_rows), :] = jnp.dot(
            group, wt[...], preferred_element_type=F32
        ).astype(BF16)
        copies = []
        for step in x_order:
            to = (xi + step) % n_x
            copy = remote(
                row_part.at[pl.ds(pl.multiple_of(g * group_rows + to * STRIP, 16), STRIP)],
                row_in.at[step - 1, pl.ds(g * STRIP, STRIP)],
                row_send.at[g, step - 1],
                row_recv.at[g, step - 1],
                {"tp": zh * n_x + to},
            )
            copy.start()
            copies.append(copy)
            finish.append(copy.wait_send)
        return copies

    def feature_cross(g, copies):
        inside = pl.ds(g * STRIP, STRIP)
        for copy in copies:
            copy.wait_recv()
        summed = row_part[
            pl.ds(pl.multiple_of(g * group_rows + xi * STRIP, 16), STRIP), :
        ].astype(F32)
        for step in range(1, n_x):
            summed = summed + row_in[step - 1, inside, :].astype(F32)
        cross_out[inside, :] = summed.astype(BF16)
        copy = remote(
            cross_out.at[inside],
            cross_in.at[inside],
            cross_send.at[g],
            cross_recv.at[g],
            {"tp": (t + n_x) % n_tp},
        )
        copy.start()
        finish.append(copy.wait_send)
        return copy

    def feature_spread(g, copy):
        inside = pl.ds(g * STRIP, STRIP)
        copy.wait_recv()
        place = strip_row(g, xi)
        fg_all[place, :] = (
            cross_out[inside, :].astype(F32) + cross_in[inside, :].astype(F32)
        ).astype(BF16)
        copies = []
        for step in x_order:
            to = {"tp": zh * n_x + (xi + step) % n_x}
            sems = full_send.at[g, step - 1], full_recv.at[g, step - 1]
            send = remote(fg_all.at[place], fg_all.at[place], *sems, to)
            send.start()
            finish.append(send.wait_send)
            landed = fg_all.at[strip_row(g, (xi + n_x - step) % n_x)]
            copies.append(remote(landed, landed, *sems, to))
        return copies

    def line_copy(out, into, send_sem, recv_sem, at, h, to):
        return remote(
            out.at[at, h], into.at[at, h], send_sem.at[at, h], recv_sem.at[at, h], {"vis": to}
        )

    right = jnp.minimum(v + 2, n_vis - 2 + core)
    left = jnp.maximum(v - 2, core)

    def pair_sum(at, h):
        span = pl.ds(pl.multiple_of(at * chunk, 16), chunk)
        return own_part[h, span, :].astype(F32) + sib_in[h, span, :].astype(F32)

    def line_step(tau, halves=range(HALVES)):
        for h in halves:

            @pl.when((z <= tau) & (z < n_z - 1) & (tau < n_z - 1))
            def _():
                at = n_z - 1 - tau + z
                copy = line_copy(right_out, right_in, right_send, right_recv, at, h, right)

                @pl.when(z > 0)
                def _():
                    copy.wait_recv()
                    right_out[at, h] = (
                        pair_sum(at, h) + right_in[at, h].astype(F32)
                    ).astype(BF16)

                @pl.when(z == 0)
                def _():
                    right_out[at, h] = pair_sum(at, h).astype(BF16)

                copy.start()

            @pl.when((n_z - 1 - z <= tau) & (z > 0) & (tau < n_z - 1))
            def _():
                at = tau - (n_z - 1 - z)
                copy = line_copy(left_out, left_in, left_send, left_recv, at, h, left)

                @pl.when(z < n_z - 1)
                def _():
                    copy.wait_recv()
                    left_out[at, h] = (
                        pair_sum(at, h) + left_in[at, h].astype(F32)
                    ).astype(BF16)

                @pl.when(z == n_z - 1)
                def _():
                    left_out[at, h] = pair_sum(at, h).astype(BF16)

                copy.start()

    def line_last():
        for h in range(HALVES):
            span = pl.ds(h * half, half)
            from_left = line_copy(right_out, right_in, right_send, right_recv, z, h, right)
            from_right = line_copy(left_out, left_in, left_send, left_recv, z, h, left)

            @pl.when(z > 0)
            def _():
                from_left.wait_recv()

            @pl.when(z < n_z - 1)
            def _():
                from_right.wait_recv()

            @pl.when(z == 0)
            def _():
                wg_ref[:, span] = (pair_sum(z, h) + left_in[z, h].astype(F32)).astype(BF16)

            @pl.when(z == n_z - 1)
            def _():
                wg_ref[:, span] = (pair_sum(z, h) + right_in[z, h].astype(F32)).astype(BF16)

            @pl.when((z > 0) & (z < n_z - 1))
            def _():
                wg_ref[:, span] = (
                    pair_sum(z, h) + right_in[z, h].astype(F32) + left_in[z, h].astype(F32)
                ).astype(BF16)

    def line_sent():
        for h in range(HALVES):

            def right_done(at, carry):
                line_copy(right_out, right_in, right_send, right_recv, at, h, right).wait_send()
                return carry

            def left_done(at, carry):
                line_copy(left_out, left_in, left_send, left_recv, at, h, left).wait_send()
                return carry

            lax.fori_loop(z + 1, n_z, right_done, 0)
            lax.fori_loop(0, z, left_done, 0)

    row_copies, cross, spread_copies = [], [], []
    send_grads(0)
    send_grads(1)
    row_copies.append(feature_products(0))
    grads_gone(0)
    send_grads(2)
    grads_here(0)
    row_copies.append(feature_products(1))
    grads_gone(1)
    send_grads(3)
    cross.append(feature_cross(0, row_copies[0]))
    grads_here(1)
    row_copies.append(feature_products(2))
    cross.append(feature_cross(1, row_copies[1]))
    grads_here(2)
    share_out(0)
    share_own(0)
    cross.append(feature_cross(2, row_copies[2]))
    sib_copies[0].wait_recv()
    line_step(0, (0,))
    grads_here(3)
    share_out(1)
    share_own(1)
    row_copies.append(feature_products(3))
    row_copies.append(feature_products(4))
    row_copies.append(feature_products(5))
    sib_copies[1].wait_recv()
    line_step(0, (1,))
    spread_copies += feature_spread(0, cross[0])
    cross.append(feature_cross(3, row_copies[3]))
    line_step(1)
    spread_copies += feature_spread(1, cross[1])
    cross.append(feature_cross(4, row_copies[4]))
    line_step(2)
    spread_copies += feature_spread(2, cross[2])
    cross.append(feature_cross(5, row_copies[5]))
    line_step(3)
    line_step(4)
    spread_copies += feature_spread(3, cross[3])
    line_step(5)
    spread_copies += feature_spread(4, cross[4])
    line_step(6)
    spread_copies += feature_spread(5, cross[5])
    line_last()
    for copy in spread_copies:
        copy.wait_recv()
    fg_ref[...] = fg_all[...]
    line_sent()
    grads_gone(2)
    grads_gone(3)
    for wait in finish:
        wait()


def hand_on(fg_in, wg_in, fg_ref, wg_ref, fg_held, wg_held, sems_in, sems_out):
    pieces = sems_in.shape[0] - 1
    size = fg_in.shape[0] // pieces
    spans = [pl.ds(at * size, size) for at in range(pieces)]
    sources = [fg_in.at[span] for span in spans] + [wg_in]
    held = [fg_held.at[span] for span in spans] + [wg_held]
    targets = [fg_ref.at[span] for span in spans] + [wg_ref]
    into = [pltpu.make_async_copy(a, b, sems_in.at[k]) for k, (a, b) in enumerate(zip(sources, held))]
    out = [pltpu.make_async_copy(a, b, sems_out.at[k]) for k, (a, b) in enumerate(zip(held, targets))]
    for copy in into:
        copy.start()
    for first, second in zip(into, out):
        first.wait()
        second.start()
    for copy in out:
        copy.wait()


def on_device(features, merge_weight, gain, positions, cotangent):
    rows, sub_count, width = features.shape
    cols = merge_weight.shape[2]
    n_vis, n_tp, n_dp = (lax.axis_size(name) for name in ("vis", "tp", "dp"))
    blocks = n_vis * n_dp
    per_block = rows // n_dp
    slots_dev = cotangent.shape[0]
    groups = cols // LANES
    tile = CAP * groups
    n_x, n_z = n_tp // 2, n_vis // 2
    half = cols // HALVES
    chunk = width // n_vis
    share = width // 2
    part_rows = rows // n_x
    n_groups = part_rows // STRIP
    vmem = pl.BlockSpec(memory_space=pltpu.VMEM)
    dma = pltpu.SemaphoreType.DMA
    feature_grad, weight_grad = pl.pallas_call(
        functools.partial(kernel, (n_vis, n_tp, n_dp)),
        out_shape=(
            jax.ShapeDtypeStruct((rows, width), BF16),
            jax.ShapeDtypeStruct((chunk, cols), BF16),
        ),
        in_specs=[vmem] * 5,
        out_specs=(vmem, vmem),
        scratch_shapes=[
            pltpu.VMEM((blocks * tile, LANES), F32),
            pltpu.VMEM((blocks, tile, LANES), BF16),
            pltpu.VMEM((blocks, tile, LANES), BF16),
            pltpu.VMEM((rows, cols), BF16),
            pltpu.VMEM((n_dp - 1, per_block, cols), BF16),
            pltpu.VMEM((per_block, cols), F32),
            pltpu.VMEM((per_block, cols), F32),
            pltpu.VMEM((LANES, LANES), F32),
            pltpu.VMEM((8, LANES), F32),
            pltpu.VMEM((n_tp, 8, LANES), F32),
            pltpu.VMEM((rows, cols), BF16),
            pltpu.VMEM((width, rows), BF16),
            pltpu.VMEM((2, share, rows), BF16),
            pltpu.VMEM((cols, width), BF16),
            pltpu.VMEM((HALVES, share, half), BF16),
            pltpu.VMEM((HALVES, share, half), BF16),
            pltpu.VMEM((HALVES, share, half), BF16),
            pltpu.VMEM((n_z, HALVES, chunk, half), BF16),
            pltpu.VMEM((n_z, HALVES, chunk, half), BF16),
            pltpu.VMEM((n_z, HALVES, chunk, half), BF16),
            pltpu.VMEM((n_z, HALVES, chunk, half), BF16),
            pltpu.VMEM((rows, width), BF16),
            pltpu.VMEM((n_x - 1, part_rows, width), BF16),
            pltpu.VMEM((part_rows, width), BF16),
            pltpu.VMEM((part_rows, width), BF16),
            pltpu.VMEM((rows, width), BF16),
            dma,
            dma,
            dma((HALVES, n_dp - 1)),
            dma((HALVES, n_dp - 1)),
            dma((n_tp - 1,)),
            dma((n_tp - 1,)),
            dma((SENDS, n_dp - 1)),
            dma((SENDS, n_dp - 1)),
            dma((HALVES,)),
            dma((HALVES,)),
            dma((n_z, HALVES)),
            dma((n_z, HALVES)),
            dma((n_z, HALVES)),
            dma((n_z, HALVES)),
            dma((n_groups, n_x - 1)),
            dma((n_groups, n_x - 1)),
            dma((n_groups,)),
            dma((n_groups,)),
            dma((n_groups, n_x - 1)),
            dma((n_groups, n_x - 1)),
        ],
        compiler_params=pltpu.CompilerParams(
            collective_id=0, has_side_effects=True, vmem_limit_bytes=56 << 20
        ),
        cost_estimate=pl.CostEstimate(
            flops=6 * rows * width * cols, bytes_accessed=6 * width * cols, transcendentals=LANES
        ),
    )(
        features.reshape(rows, width),
        merge_weight.reshape(width, cols),
        gain.reshape(1, cols),
        positions.reshape(-1, LANES),
        cotangent,
    )
    anywhere = pl.BlockSpec(memory_space=pl.ANY)
    feature_grad, weight_grad = pl.pallas_call(
        hand_on,
        out_shape=(
            jax.ShapeDtypeStruct((rows, width), BF16),
            jax.ShapeDtypeStruct((chunk, cols), BF16),
        ),
        in_specs=[anywhere] * 2,
        out_specs=(anywhere, anywhere),
        scratch_shapes=[
            pltpu.VMEM((rows, width), BF16),
            pltpu.VMEM((chunk, cols), BF16),
            dma((PIECES + 1,)),
            dma((PIECES + 1,)),
        ],
        compiler_params=pltpu.CompilerParams(vmem_limit_bytes=60 << 20),
    )(feature_grad, weight_grad)
    return (feature_grad.reshape(features.shape), weight_grad.reshape(1, chunk, cols))


def solution(mesh):
    return jax.shard_map(
        on_device,
        mesh=mesh,
        in_specs=(P("vis", "dp", None), P("dp", None, "tp"), P("tp"), P(), P(("vis", "dp"), "tp")),
        out_specs=(P("vis", "dp", None), P("dp", "vis", "tp")),
        check_vma=False,
    )
```

```python
import functools

import jax
import jax.numpy as jnp
from jax import lax
from jax.experimental import pallas as pl
from jax.experimental.pallas import tpu as pltpu
from jax.sharding import PartitionSpec as P

MESH = pl.DeviceIdType.MESH
F32 = jnp.float32
BF16 = jnp.bfloat16
EPS = 1e-06
LANES = 128
CAP = 2
HALVES = 2
FINE = 2
STRIP = 16
SENDS = 4
PIECES = 4


def remote(src, dst, send_sem, recv_sem, device):
    return pltpu.make_async_remote_copy(
        src_ref=src,
        dst_ref=dst,
        send_sem=send_sem,
        recv_sem=recv_sem,
        device_id=device,
        device_id_type=MESH,
    )


def kernel(
    sizes,
    x_hbm,
    w_hbm,
    gain_ref,
    pos_ref,
    cot_ref,
    fg_ref,
    wg_ref,
    x_ref,
    w_ref,
    slots_wide,
    a2a_out,
    a2a_in,
    term,
    term_in,
    vals,
    scaled,
    stat_tile,
    stat_out,
    stat_in,
    grads,
    xt_plain,
    xt,
    wt,
    own_part,
    sib_out,
    sib_in,
    right_out,
    right_in,
    left_out,
    left_in,
    row_part,
    row_in,
    cross_out,
    cross_in,
    fg_all,
    a2a_send,
    a2a_recv,
    term_send,
    term_recv,
    stat_send,
    stat_recv,
    grad_send,
    grad_recv,
    sib_send,
    sib_recv,
    right_send,
    right_recv,
    left_send,
    left_recv,
    row_send,
    row_recv,
    cross_send,
    cross_recv,
    full_send,
    full_recv,
    load_sems,
    store_sems,
):
    n_vis, n_tp, n_dp = sizes
    n_x = n_tp // 2
    n_z = n_vis // 2
    blocks = n_vis * n_dp
    rows = x_ref.shape[0]
    width = x_ref.shape[1]
    cols = w_ref.shape[1]
    per_block = rows // n_dp
    groups = cols // LANES
    slots_dev = cot_ref.shape[0]
    tile = CAP * groups
    total_cols = cols * n_tp
    half = cols // HALVES
    chunk = width // n_vis

    v = lax.axis_index("vis")
    t = lax.axis_index("tp")
    d = lax.axis_index("dp")
    z, core = v // 2, v % 2
    zh, xi = t // n_x, t % n_x
    me = v * n_dp + d

    def block_device(block):
        return {"vis": block // n_dp, "dp": block % n_dp}

    loads = [
        pltpu.make_async_copy(x_hbm, x_ref, load_sems.at[0]),
        pltpu.make_async_copy(w_hbm, w_ref, load_sems.at[1]),
    ]
    for load in loads:
        load.start()

    barrier = pltpu.get_barrier_semaphore()

    def greet(step, carry):
        pl.semaphore_signal(
            barrier, inc=1, device_id=block_device((me + step) % blocks), device_id_type=MESH
        )
        return carry

    for step in range(1, n_tp):
        pl.semaphore_signal(
            barrier, inc=1, device_id={"tp": (t + step) % n_tp}, device_id_type=MESH
        )
    lax.fori_loop(1, blocks, greet, 0)

    here = lax.broadcasted_iota(jnp.int32, (slots_dev, LANES), 0) + me * slots_dev
    block_at = jnp.full((slots_dev, LANES), -1, jnp.int32)
    for line in range(pos_ref.shape[0]):
        block_at = jnp.where(pos_ref[line : line + 1, :] == here, line, block_at)
    lane_at = lax.broadcasted_iota(jnp.int32, (slots_dev, LANES), 1)
    block_at = jnp.where(block_at < 0, -1, (block_at * LANES + lane_at) // per_block)
    block_sub = jnp.broadcast_to(
        jnp.max(block_at.astype(F32), axis=1, keepdims=True), (slots_dev, LANES)
    )
    block_lane = block_sub.T
    first = lax.broadcasted_iota(jnp.int32, (LANES, LANES), 0)
    second = lax.broadcasted_iota(jnp.int32, (LANES, LANES), 1)
    earlier = jnp.where((block_sub == block_lane) & (first < second), 1.0, 0.0)
    rank = jnp.sum(earlier, axis=0, keepdims=True)
    slot = jnp.where(block_lane[0:1, :] < 0.0, -8192.0, block_lane[0:1, :] * CAP + rank)
    slot_row = slot.astype(jnp.int32)
    pick = jnp.where(
        lax.broadcasted_iota(jnp.int32, (blocks * CAP, LANES), 0) == slot_row, 1.0, 0.0
    ).astype(BF16)
    for group in range(groups):
        slots_wide[pl.ds(group, blocks * CAP, stride=groups), :] = jnp.dot(
            pick, cot_ref[:, pl.ds(group * LANES, LANES)], preferred_element_type=F32
        )
    a2a_out[...] = slots_wide[...].astype(BF16).reshape(blocks, tile, LANES)
    a2a_in[pl.ds(me, 1)] = a2a_out[pl.ds(me, 1)]

    pl.semaphore_wait(barrier, blocks - 1 + n_tp - 1)

    def send_slots(step, carry):
        block = (me + step) % blocks
        remote(
            a2a_out.at[block], a2a_in.at[me], a2a_send, a2a_recv, block_device(block)
        ).start()
        return carry

    lax.fori_loop(1, blocks, send_slots, 0)
    others = pl.ds(0, blocks - 1)
    a2a_all = remote(
        a2a_out.at[others], a2a_in.at[others], a2a_send, a2a_recv, block_device((me + 1) % blocks)
    )
    finish = [a2a_all.wait_send]

    for load in loads:
        load.wait()

    order = [s for s in range(1, n_dp)]
    order.sort(key=lambda s: -min(s, n_dp - s))
    term_copies = []
    for h in range(HALVES):
        span = pl.ds(h * half, half)
        term[:, span] = jnp.dot(
            x_ref[...], w_ref[:, span], preferred_element_type=F32
        ).astype(BF16)
        for step in order:
            to = (d + step) % n_dp
            copy = remote(
                term.at[pl.ds(pl.multiple_of(to * per_block, 16), per_block), span],
                term_in.at[step - 1, :, span],
                term_send.at[h, step - 1],
                term_recv.at[h, step - 1],
                {"dp": to},
            )
            copy.start()
            term_copies.append(copy)
            finish.append(copy.wait_send)

    for start in range(0, width, LANES):
        xt_plain[pl.ds(start, LANES), :] = x_ref[:, pl.ds(start, LANES)].T
    for at in range(n_vis):
        xt[at % 2, pl.ds((at // 2) * chunk, chunk), :] = xt_plain[pl.ds(at * chunk, chunk), :]

    for start in range(0, cols, LANES):
        wt[pl.ds(start, LANES), :] = w_ref[:, pl.ds(start, LANES)].T

    flat = lax.broadcasted_iota(jnp.int32, (LANES, LANES), 0) + me * per_block
    line_first = (me * per_block) // LANES
    line_next = jnp.minimum(line_first + 1, pos_ref.shape[0] - 1)
    line_pos = jnp.where(
        flat // LANES == line_first, pos_ref[pl.ds(line_first, 1), :], pos_ref[pl.ds(line_next, 1), :]
    )
    row_pos = jnp.sum(
        jnp.where(flat % LANES == second, line_pos, 0).astype(F32), axis=1, keepdims=True
    )
    row_pos = jnp.where(first[:, 0:1] < per_block, row_pos, -1.0)
    pos_sub = jnp.broadcast_to(row_pos, (LANES, LANES))
    owner_sub = jnp.floor(pos_sub / slots_dev)
    pos_lane = pos_sub.T
    owner_lane = owner_sub.T
    before = jnp.where((owner_sub == owner_lane) & (pos_lane < pos_sub), 1.0, 0.0)
    row_slot = owner_sub[:, 0:1] * CAP + jnp.sum(before, axis=1, keepdims=True)
    in_slot = lax.broadcasted_iota(jnp.int32, (per_block, blocks * CAP), 1)
    select = jnp.where(
        in_slot == row_slot[0:per_block].astype(jnp.int32), 1.0, 0.0
    ).astype(BF16)

    a2a_all.wait_recv()
    slots_wide[...] = a2a_in[...].reshape(blocks * tile, LANES).astype(F32)
    for group in range(groups):
        span = pl.ds(group * LANES, LANES)
        arrived = slots_wide[pl.ds(group, blocks * CAP, stride=groups), :].astype(BF16)
        scaled[:, span] = (
            jnp.dot(select, arrived, preferred_element_type=F32) * gain_ref[:, span]
        )

    for copy in term_copies:
        copy.wait_recv()
    mine = pl.ds(pl.multiple_of(d * per_block, 16), per_block)
    total = term[mine, :].astype(F32)
    for step in range(1, n_dp):
        total = total + term_in[step - 1].astype(F32)
    value = total.astype(BF16).astype(F32)
    vals[...] = value
    square = jnp.sum(value * value, axis=1, keepdims=True)
    dotted = jnp.sum(scaled[...] * value, axis=1, keepdims=True)

    lane = lax.broadcasted_iota(jnp.int32, (per_block, LANES), 1)
    stat_tile[...] = jnp.zeros_like(stat_tile)
    stat_tile[0:per_block, :] = jnp.where(lane == 0, square, jnp.where(lane == 1, dotted, 0.0))
    stat_out[...] = stat_tile[...].T[0:8, :]
    stat_in[pl.ds(t, 1)] = stat_out[...].reshape(1, 8, LANES)
    stat_copies = []
    for step in sorted(range(1, n_tp), key=lambda s: -(s == n_x)):
        copy = remote(
            stat_out,
            stat_in.at[t],
            stat_send.at[step - 1],
            stat_recv.at[step - 1],
            {"tp": (t + step) % n_tp},
        )
        copy.start()
        stat_copies.append(copy)
        finish.append(copy.wait_send)
    for copy in stat_copies:
        copy.wait_recv()
    sums = stat_in[0]
    for at in range(1, n_tp):
        sums = sums + stat_in[at]
    inverse = lax.rsqrt(sums[0:1, :] / total_cols + EPS)
    factor = inverse * inverse * inverse * (sums[1:2, :] / total_cols)
    sub = lax.broadcasted_iota(jnp.int32, (LANES, LANES), 0)
    spread = jnp.where(sub == 0, inverse, jnp.where(sub == 1, factor, 0.0)).T
    inverse_col = spread[0:per_block, 0:1]
    factor_col = spread[0:per_block, 1:2]

    rest = per_block - 2 * STRIP
    sends = (
        (0, STRIP, pl.ds(0, cols)),
        (STRIP, STRIP, pl.ds(0, cols)),
        (2 * STRIP, rest, pl.ds(0, half)),
        (2 * STRIP, rest, pl.ds(half, half)),
    )
    grads[mine, :] = (inverse_col * scaled[...] - factor_col * vals[...]).astype(BF16)
    grad_copies = []
    grad_sent = []

    def send_grads(g):
        at, size, span = sends[g]
        group = pl.ds(pl.multiple_of(d * per_block + at, 16), size)
        arrivals, sent = {}, []
        for step in order:
            to = {"dp": (d + step) % n_dp}
            sems = grad_send.at[g, step - 1], grad_recv.at[g, step - 1]
            copy = remote(grads.at[group, span], grads.at[group, span], *sems, to)
            copy.start()
            sent.append(copy.wait_send)
            source = (d + n_dp - step) % n_dp
            landed = grads.at[
                pl.ds(pl.multiple_of(source * per_block + at, 16), size), span
            ]
            arrivals[step] = remote(landed, landed, *sems, to)
        grad_copies.append(arrivals)
        grad_sent.append(sent)

    def grads_here(g):
        for copy in grad_copies[g].values():
            copy.wait_recv()

    def grads_gone(g):
        for wait in grad_sent[g]:
            wait()

    sib_copies = []

    def share_out(h):
        span = pl.ds(h * half, half)
        sib_out[h] = jnp.dot(
            xt[1 - core], grads[:, span], preferred_element_type=F32
        ).astype(BF16)
        copy = remote(
            sib_out.at[h],
            sib_in.at[h],
            sib_send.at[h],
            sib_recv.at[h],
            {"vis": v + 1 - 2 * core},
        )
        copy.start()
        sib_copies.append(copy)
        finish.append(copy.wait_send)

    def share_own(h):
        span = pl.ds(h * half, half)
        own_part[h] = jnp.dot(xt[core], grads[:, span], preferred_element_type=F32).astype(BF16)

    x_order = sorted(range(1, n_x), key=lambda s: -min(s, n_x - s))
    group_rows = STRIP * n_x

    def strip_row(g, at):
        if g == 0:
            row = d * per_block + at * STRIP
        elif g < 3:
            row = jnp.where(
                at == 0,
                d * per_block + group_rows + (g - 1) * STRIP,
                ((d + at) % n_dp) * per_block + (g - 1) * STRIP,
            )
        else:
            row = ((d + g - 2) % n_dp) * per_block + 2 * STRIP + at * STRIP
        return pl.ds(pl.multiple_of(row, 16), STRIP)

    def feature_products(g):
        group = jnp.concatenate([grads[strip_row(g, at), :] for at in range(n_x)], axis=0)
        row_part[pl.ds(g * group_rows, group_rows), :] = jnp.dot(
            group, wt[...], preferred_element_type=F32
        ).astype(BF16)
        copies = []
        for step in x_order:
            to = (xi + step) % n_x
            copy = remote(
                row_part.at[pl.ds(pl.multiple_of(g * group_rows + to * STRIP, 16), STRIP)],
                row_in.at[step - 1, pl.ds(g * STRIP, STRIP)],
                row_send.at[g, step - 1],
                row_recv.at[g, step - 1],
                {"tp": zh * n_x + to},
            )
            copy.start()
            copies.append(copy)
            finish.append(copy.wait_send)
        return copies

    def feature_cross(g, copies):
        inside = pl.ds(g * STRIP, STRIP)
        for copy in copies:
            copy.wait_recv()
        summed = row_part[
            pl.ds(pl.multiple_of(g * group_rows + xi * STRIP, 16), STRIP), :
        ].astype(F32)
        for step in range(1, n_x):
            summed = summed + row_in[step - 1, inside, :].astype(F32)
        cross_out[inside, :] = summed.astype(BF16)
        copy = remote(
            cross_out.at[inside],
            cross_in.at[inside],
            cross_send.at[g],
            cross_recv.at[g],
            {"tp": (t + n_x) % n_tp},
        )
        copy.start()
        finish.append(copy.wait_send)
        return copy

    def feature_spread(g, copy):
        inside = pl.ds(g * STRIP, STRIP)
        copy.wait_recv()
        place = strip_row(g, xi)
        fg_all[place, :] = (
            cross_out[inside, :].astype(F32) + cross_in[inside, :].astype(F32)
        ).astype(BF16)
        copies = []
        for step in x_order:
            to = {"tp": zh * n_x + (xi + step) % n_x}
            sems = full_send.at[g, step - 1], full_recv.at[g, step - 1]
            send = remote(fg_all.at[place], fg_all.at[place], *sems, to)
            send.start()
            finish.append(send.wait_send)
            landed = fg_all.at[strip_row(g, (xi + n_x - step) % n_x)]
            copies.append(remote(landed, landed, *sems, to))
        return copies

    def line_copy(out, into, send_sem, recv_sem, at, h, to):
        return remote(
            out.at[at, h], into.at[at, h], send_sem.at[at, h], recv_sem.at[at, h], {"vis": to}
        )

    right = jnp.minimum(v + 2, n_vis - 2 + core)
    left = jnp.maximum(v - 2, core)

    fine = half // FINE

    def pair_sum(at, q):
        span = pl.ds(pl.multiple_of(at * chunk, 16), chunk)
        h, inner = q // FINE, pl.ds(q % FINE * fine, fine)
        return own_part[h, span, inner].astype(F32) + sib_in[h, span, inner].astype(F32)

    def line_step(tau, halves=range(HALVES)):
        for h in [x * FINE + y for x in halves for y in range(FINE)]:

            @pl.when((z <= tau) & (z < n_z - 1) & (tau < n_z - 1))
            def _():
                at = n_z - 1 - tau + z
                copy = line_copy(right_out, right_in, right_send, right_recv, at, h, right)

                @pl.when(z > 0)
                def _():
                    copy.wait_recv()
                    right_out[at, h] = (
                        pair_sum(at, h) + right_in[at, h].astype(F32)
                    ).astype(BF16)

                @pl.when(z == 0)
                def _():
                    right_out[at, h] = pair_sum(at, h).astype(BF16)

                copy.start()

            @pl.when((n_z - 1 - z <= tau) & (z > 0) & (tau < n_z - 1))
            def _():
                at = tau - (n_z - 1 - z)
                copy = line_copy(left_out, left_in, left_send, left_recv, at, h, left)

                @pl.when(z < n_z - 1)
                def _():
                    copy.wait_recv()
                    left_out[at, h] = (
                        pair_sum(at, h) + left_in[at, h].astype(F32)
                    ).astype(BF16)

                @pl.when(z == n_z - 1)
                def _():
                    left_out[at, h] = pair_sum(at, h).astype(BF16)

                copy.start()

    def line_last():
        for h in range(HALVES * FINE):
            span = pl.ds(h * fine, fine)
            from_left = line_copy(right_out, right_in, right_send, right_recv, z, h, right)
            from_right = line_copy(left_out, left_in, left_send, left_recv, z, h, left)

            @pl.when(z > 0)
            def _():
                from_left.wait_recv()

            @pl.when(z < n_z - 1)
            def _():
                from_right.wait_recv()

            @pl.when(z == 0)
            def _():
                wg_ref[:, span] = (pair_sum(z, h) + left_in[z, h].astype(F32)).astype(BF16)

            @pl.when(z == n_z - 1)
            def _():
                wg_ref[:, span] = (pair_sum(z, h) + right_in[z, h].astype(F32)).astype(BF16)

            @pl.when((z > 0) & (z < n_z - 1))
            def _():
                wg_ref[:, span] = (
                    pair_sum(z, h) + right_in[z, h].astype(F32) + left_in[z, h].astype(F32)
                ).astype(BF16)

    def line_sent():
        for h in range(HALVES * FINE):

            def right_done(at, carry):
                line_copy(right_out, right_in, right_send, right_recv, at, h, right).wait_send()
                return carry

            def left_done(at, carry):
                line_copy(left_out, left_in, left_send, left_recv, at, h, left).wait_send()
                return carry

            lax.fori_loop(z + 1, n_z, right_done, 0)
            lax.fori_loop(0, z, left_done, 0)

    row_copies, cross, spread_copies = [], [], []
    send_grads(0)
    send_grads(1)
    row_copies.append(feature_products(0))
    grads_gone(0)
    send_grads(2)
    grads_here(0)
    row_copies.append(feature_products(1))
    grads_gone(1)
    send_grads(3)
    cross.append(feature_cross(0, row_copies[0]))
    grads_here(1)
    row_copies.append(feature_products(2))
    cross.append(feature_cross(1, row_copies[1]))
    grads_here(2)
    share_out(0)
    share_own(0)
    cross.append(feature_cross(2, row_copies[2]))
    sib_copies[0].wait_recv()
    line_step(0, (0,))
    grads_here(3)
    share_out(1)
    share_own(1)
    row_copies.append(feature_products(3))
    row_copies.append(feature_products(4))
    row_copies.append(feature_products(5))
    sib_copies[1].wait_recv()
    line_step(0, (1,))
    spread_copies += feature_spread(0, cross[0])
    cross.append(feature_cross(3, row_copies[3]))
    spread_copies += feature_spread(1, cross[1])
    line_step(1)
    cross.append(feature_cross(4, row_copies[4]))
    spread_copies += feature_spread(2, cross[2])
    cross.append(feature_cross(5, row_copies[5]))
    line_step(2)
    spread_copies += feature_spread(3, cross[3])
    line_step(3)
    spread_copies += feature_spread(4, cross[4])
    line_step(4)
    spread_copies += feature_spread(5, cross[5])
    line_step(5)
    for copy in spread_copies:
        copy.wait_recv()
    pieces = store_sems.shape[0]
    size = rows // pieces
    stores = [
        pltpu.make_async_copy(
            fg_all.at[pl.ds(k * size, size)], fg_ref.at[pl.ds(k * size, size)], store_sems.at[k]
        )
        for k in range(pieces)
    ]
    for store in stores:
        store.start()
    line_step(6)
    line_last()
    for store in stores:
        store.wait()
    line_sent()
    grads_gone(2)
    grads_gone(3)
    for wait in finish:
        wait()


def hand_on(fg_in, wg_in, fg_ref, wg_ref, fg_held, wg_held, sems_in, sems_out):
    pieces = sems_in.shape[0] - 1
    size = fg_in.shape[0] // pieces
    spans = [pl.ds(at * size, size) for at in range(pieces)]
    sources = [fg_in.at[span] for span in spans] + [wg_in]
    held = [fg_held.at[span] for span in spans] + [wg_held]
    targets = [fg_ref.at[span] for span in spans] + [wg_ref]
    into = [pltpu.make_async_copy(a, b, sems_in.at[k]) for k, (a, b) in enumerate(zip(sources, held))]
    out = [pltpu.make_async_copy(a, b, sems_out.at[k]) for k, (a, b) in enumerate(zip(held, targets))]
    for copy in into:
        copy.start()
    for first, second in zip(into, out):
        first.wait()
        second.start()
    for copy in out:
        copy.wait()


def on_device(features, merge_weight, gain, positions, cotangent):
    rows, sub_count, width = features.shape
    cols = merge_weight.shape[2]
    n_vis, n_tp, n_dp = (lax.axis_size(name) for name in ("vis", "tp", "dp"))
    blocks = n_vis * n_dp
    per_block = rows // n_dp
    slots_dev = cotangent.shape[0]
    groups = cols // LANES
    tile = CAP * groups
    n_x, n_z = n_tp // 2, n_vis // 2
    half = cols // HALVES
    chunk = width // n_vis
    share = width // 2
    part_rows = rows // n_x
    n_groups = part_rows // STRIP
    vmem = pl.BlockSpec(memory_space=pltpu.VMEM)
    anywhere = pl.BlockSpec(memory_space=pl.ANY)
    dma = pltpu.SemaphoreType.DMA
    feature_grad, weight_grad = pl.pallas_call(
        functools.partial(kernel, (n_vis, n_tp, n_dp)),
        out_shape=(
            jax.ShapeDtypeStruct((rows, width), BF16),
            jax.ShapeDtypeStruct((chunk, cols), BF16),
        ),
        in_specs=[anywhere] * 2 + [vmem] * 3,
        out_specs=(anywhere, vmem),
        scratch_shapes=[
            pltpu.VMEM((rows, width), BF16),
            pltpu.VMEM((width, cols), BF16),
            pltpu.VMEM((blocks * tile, LANES), F32),
            pltpu.VMEM((blocks, tile, LANES), BF16),
            pltpu.VMEM((blocks, tile, LANES), BF16),
            pltpu.VMEM((rows, cols), BF16),
            pltpu.VMEM((n_dp - 1, per_block, cols), BF16),
            pltpu.VMEM((per_block, cols), F32),
            pltpu.VMEM((per_block, cols), F32),
            pltpu.VMEM((LANES, LANES), F32),
            pltpu.VMEM((8, LANES), F32),
            pltpu.VMEM((n_tp, 8, LANES), F32),
            pltpu.VMEM((rows, cols), BF16),
            pltpu.VMEM((width, rows), BF16),
            pltpu.VMEM((2, share, rows), BF16),
            pltpu.VMEM((cols, width), BF16),
            pltpu.VMEM((HALVES, share, half), BF16),
            pltpu.VMEM((HALVES, share, half), BF16),
            pltpu.VMEM((HALVES, share, half), BF16),
            pltpu.VMEM((n_z, HALVES * FINE, chunk, half // FINE), BF16),
            pltpu.VMEM((n_z, HALVES * FINE, chunk, half // FINE), BF16),
            pltpu.VMEM((n_z, HALVES * FINE, chunk, half // FINE), BF16),
            pltpu.VMEM((n_z, HALVES * FINE, chunk, half // FINE), BF16),
            pltpu.VMEM((rows, width), BF16),
            pltpu.VMEM((n_x - 1, part_rows, width), BF16),
            pltpu.VMEM((part_rows, width), BF16),
            pltpu.VMEM((part_rows, width), BF16),
            pltpu.VMEM((rows, width), BF16),
            dma,
            dma,
            dma((HALVES, n_dp - 1)),
            dma((HALVES, n_dp - 1)),
            dma((n_tp - 1,)),
            dma((n_tp - 1,)),
            dma((SENDS, n_dp - 1)),
            dma((SENDS, n_dp - 1)),
            dma((HALVES,)),
            dma((HALVES,)),
            dma((n_z, HALVES * FINE)),
            dma((n_z, HALVES * FINE)),
            dma((n_z, HALVES * FINE)),
            dma((n_z, HALVES * FINE)),
            dma((n_groups, n_x - 1)),
            dma((n_groups, n_x - 1)),
            dma((n_groups,)),
            dma((n_groups,)),
            dma((n_groups, n_x - 1)),
            dma((n_groups, n_x - 1)),
            dma((2,)),
            dma((n_groups,)),
        ],
        compiler_params=pltpu.CompilerParams(
            collective_id=0, has_side_effects=True, vmem_limit_bytes=56 << 20
        ),
        cost_estimate=pl.CostEstimate(
            flops=6 * rows * width * cols, bytes_accessed=6 * width * cols, transcendentals=LANES
        ),
    )(
        features.reshape(rows, width),
        merge_weight.reshape(width, cols),
        gain.reshape(1, cols),
        positions.reshape(-1, LANES),
        cotangent,
    )
    feature_grad, weight_grad = pl.pallas_call(
        hand_on,
        out_shape=(
            jax.ShapeDtypeStruct((rows, width), BF16),
            jax.ShapeDtypeStruct((chunk, cols), BF16),
        ),
        in_specs=[anywhere] * 2,
        out_specs=(anywhere, anywhere),
        scratch_shapes=[
            pltpu.VMEM((rows, width), BF16),
            pltpu.VMEM((chunk, cols), BF16),
            dma((PIECES + 1,)),
            dma((PIECES + 1,)),
        ],
        compiler_params=pltpu.CompilerParams(vmem_limit_bytes=60 << 20),
    )(feature_grad, weight_grad)
    return (feature_grad.reshape(features.shape), weight_grad.reshape(1, chunk, cols))


def solution(mesh):
    return jax.shard_map(
        on_device,
        mesh=mesh,
        in_specs=(P("vis", "dp", None), P("dp", None, "tp"), P("tp"), P(), P(("vis", "dp"), "tp")),
        out_specs=(P("vis", "dp", None), P("dp", "vis", "tp")),
        check_vma=False,
    )
```

```python
import functools

import jax
import jax.numpy as jnp
from jax import lax
from jax.experimental import pallas as pl
from jax.experimental.pallas import tpu as pltpu
from jax.sharding import PartitionSpec as P

MESH = pl.DeviceIdType.MESH
F32 = jnp.float32
BF16 = jnp.bfloat16
EPS = 1e-06
LANES = 128
CAP = 2
HALVES = 2
FINE = 2
STRIP = 16
SENDS = 4
PIECES = 4


def remote(src, dst, send_sem, recv_sem, device):
    return pltpu.make_async_remote_copy(
        src_ref=src,
        dst_ref=dst,
        send_sem=send_sem,
        recv_sem=recv_sem,
        device_id=device,
        device_id_type=MESH,
    )


def kernel(
    sizes,
    x_hbm,
    w_hbm,
    gain_ref,
    pos_ref,
    cot_ref,
    fg_ref,
    wg_ref,
    x_ref,
    w_ref,
    slots_wide,
    a2a_out,
    a2a_in,
    term,
    term_in,
    vals,
    scaled,
    stat_tile,
    stat_out,
    stat_in,
    grads,
    xt_plain,
    xt,
    wt,
    own_part,
    sib_out,
    sib_in,
    right_out,
    right_in,
    left_out,
    left_in,
    row_part,
    row_in,
    cross_out,
    cross_in,
    fg_all,
    a2a_send,
    a2a_recv,
    term_send,
    term_recv,
    stat_send,
    stat_recv,
    grad_send,
    grad_recv,
    sib_send,
    sib_recv,
    right_send,
    right_recv,
    left_send,
    left_recv,
    row_send,
    row_recv,
    cross_send,
    cross_recv,
    full_send,
    full_recv,
    load_sems,
    store_sems,
):
    n_vis, n_tp, n_dp = sizes
    n_x = n_tp // 2
    n_z = n_vis // 2
    blocks = n_vis * n_dp
    rows = x_ref.shape[0]
    width = x_ref.shape[1]
    cols = w_ref.shape[1]
    per_block = rows // n_dp
    groups = cols // LANES
    slots_dev = cot_ref.shape[0]
    tile = CAP * groups
    total_cols = cols * n_tp
    half = cols // HALVES
    chunk = width // n_vis

    v = lax.axis_index("vis")
    t = lax.axis_index("tp")
    d = lax.axis_index("dp")
    z, core = v // 2, v % 2
    zh, xi = t // n_x, t % n_x
    me = v * n_dp + d

    def block_device(block):
        return {"vis": block // n_dp, "dp": block % n_dp}

    loads = [
        pltpu.make_async_copy(x_hbm, x_ref, load_sems.at[0]),
        pltpu.make_async_copy(w_hbm, w_ref, load_sems.at[1]),
    ]
    for load in loads:
        load.start()

    barrier = pltpu.get_barrier_semaphore()

    def greet(step, carry):
        pl.semaphore_signal(
            barrier, inc=1, device_id=block_device((me + step) % blocks), device_id_type=MESH
        )
        return carry

    for step in range(1, n_tp):
        pl.semaphore_signal(
            barrier, inc=1, device_id={"tp": (t + step) % n_tp}, device_id_type=MESH
        )
    lax.fori_loop(1, blocks, greet, 0)

    here = lax.broadcasted_iota(jnp.int32, (slots_dev, LANES), 0) + me * slots_dev
    block_at = jnp.full((slots_dev, LANES), -1, jnp.int32)
    for line in range(pos_ref.shape[0]):
        block_at = jnp.where(pos_ref[line : line + 1, :] == here, line, block_at)
    lane_at = lax.broadcasted_iota(jnp.int32, (slots_dev, LANES), 1)
    block_at = jnp.where(block_at < 0, -1, (block_at * LANES + lane_at) // per_block)
    block_sub = jnp.broadcast_to(
        jnp.max(block_at.astype(F32), axis=1, keepdims=True), (slots_dev, LANES)
    )
    block_lane = block_sub.T
    first = lax.broadcasted_iota(jnp.int32, (LANES, LANES), 0)
    second = lax.broadcasted_iota(jnp.int32, (LANES, LANES), 1)
    earlier = jnp.where((block_sub == block_lane) & (first < second), 1.0, 0.0)
    rank = jnp.sum(earlier, axis=0, keepdims=True)
    slot = jnp.where(block_lane[0:1, :] < 0.0, -8192.0, block_lane[0:1, :] * CAP + rank)
    slot_row = slot.astype(jnp.int32)
    pick = jnp.where(
        lax.broadcasted_iota(jnp.int32, (blocks * CAP, LANES), 0) == slot_row, 1.0, 0.0
    ).astype(BF16)
    for group in range(groups):
        slots_wide[pl.ds(group, blocks * CAP, stride=groups), :] = jnp.dot(
            pick, cot_ref[:, pl.ds(group * LANES, LANES)], preferred_element_type=F32
        )
    a2a_out[...] = slots_wide[...].astype(BF16).reshape(blocks, tile, LANES)
    a2a_in[pl.ds(me, 1)] = a2a_out[pl.ds(me, 1)]

    pl.semaphore_wait(barrier, blocks - 1 + n_tp - 1)

    def send_slots(step, carry):
        block = (me + step) % blocks
        remote(
            a2a_out.at[block], a2a_in.at[me], a2a_send, a2a_recv, block_device(block)
        ).start()
        return carry

    lax.fori_loop(1, blocks, send_slots, 0)
    others = pl.ds(0, blocks - 1)
    a2a_all = remote(
        a2a_out.at[others], a2a_in.at[others], a2a_send, a2a_recv, block_device((me + 1) % blocks)
    )
    finish = [a2a_all.wait_send]

    for load in loads:
        load.wait()

    order = [s for s in range(1, n_dp)]
    order.sort(key=lambda s: -min(s, n_dp - s))
    term_copies = []
    for h in range(HALVES):
        span = pl.ds(h * half, half)
        term[:, span] = jnp.dot(
            x_ref[...], w_ref[:, span], preferred_element_type=F32
        ).astype(BF16)
        for step in order:
            to = (d + step) % n_dp
            copy = remote(
                term.at[pl.ds(pl.multiple_of(to * per_block, 16), per_block), span],
                term_in.at[step - 1, :, span],
                term_send.at[h, step - 1],
                term_recv.at[h, step - 1],
                {"dp": to},
            )
            copy.start()
            term_copies.append(copy)
            finish.append(copy.wait_send)

    for start in range(0, width, LANES):
        xt_plain[pl.ds(start, LANES), :] = x_ref[:, pl.ds(start, LANES)].T
    for at in range(n_vis):
        xt[at % 2, pl.ds((at // 2) * chunk, chunk), :] = xt_plain[pl.ds(at * chunk, chunk), :]

    for start in range(0, cols, LANES):
        wt[pl.ds(start, LANES), :] = w_ref[:, pl.ds(start, LANES)].T

    flat = lax.broadcasted_iota(jnp.int32, (LANES, LANES), 0) + me * per_block
    line_first = (me * per_block) // LANES
    line_next = jnp.minimum(line_first + 1, pos_ref.shape[0] - 1)
    line_pos = jnp.where(
        flat // LANES == line_first, pos_ref[pl.ds(line_first, 1), :], pos_ref[pl.ds(line_next, 1), :]
    )
    row_pos = jnp.sum(
        jnp.where(flat % LANES == second, line_pos, 0).astype(F32), axis=1, keepdims=True
    )
    row_pos = jnp.where(first[:, 0:1] < per_block, row_pos, -1.0)
    pos_sub = jnp.broadcast_to(row_pos, (LANES, LANES))
    owner_sub = jnp.floor(pos_sub / slots_dev)
    pos_lane = pos_sub.T
    owner_lane = owner_sub.T
    before = jnp.where((owner_sub == owner_lane) & (pos_lane < pos_sub), 1.0, 0.0)
    row_slot = owner_sub[:, 0:1] * CAP + jnp.sum(before, axis=1, keepdims=True)
    in_slot = lax.broadcasted_iota(jnp.int32, (per_block, blocks * CAP), 1)
    select = jnp.where(
        in_slot == row_slot[0:per_block].astype(jnp.int32), 1.0, 0.0
    ).astype(BF16)

    a2a_all.wait_recv()
    slots_wide[...] = a2a_in[...].reshape(blocks * tile, LANES).astype(F32)
    for group in range(groups):
        span = pl.ds(group * LANES, LANES)
        arrived = slots_wide[pl.ds(group, blocks * CAP, stride=groups), :].astype(BF16)
        scaled[:, span] = (
            jnp.dot(select, arrived, preferred_element_type=F32) * gain_ref[:, span]
        )

    for copy in term_copies:
        copy.wait_recv()
    mine = pl.ds(pl.multiple_of(d * per_block, 16), per_block)
    total = term[mine, :].astype(F32)
    for step in range(1, n_dp):
        total = total + term_in[step - 1].astype(F32)
    value = total.astype(BF16).astype(F32)
    vals[...] = value
    square = jnp.sum(value * value, axis=1, keepdims=True)
    dotted = jnp.sum(scaled[...] * value, axis=1, keepdims=True)

    lane = lax.broadcasted_iota(jnp.int32, (per_block, LANES), 1)
    stat_tile[...] = jnp.zeros_like(stat_tile)
    stat_tile[0:per_block, :] = jnp.where(lane == 0, square, jnp.where(lane == 1, dotted, 0.0))
    stat_out[...] = stat_tile[...].T[0:8, :]
    stat_in[pl.ds(t, 1)] = stat_out[...].reshape(1, 8, LANES)
    stat_copies = []
    far = [(1 - zh, step, step) for step in range(n_x)]
    near = [(zh, step, n_x + step - 1) for step in range(1, n_x)]
    for side, step, at in far + near:
        copy = remote(
            stat_out,
            stat_in.at[t],
            stat_send.at[at],
            stat_recv.at[at],
            {"tp": side * n_x + (xi + step) % n_x},
        )
        copy.start()
        stat_copies.append(copy)
        finish.append(copy.wait_send)
    for copy in stat_copies:
        copy.wait_recv()
    sums = stat_in[0]
    for at in range(1, n_tp):
        sums = sums + stat_in[at]
    inverse = lax.rsqrt(sums[0:1, :] / total_cols + EPS)
    factor = inverse * inverse * inverse * (sums[1:2, :] / total_cols)
    sub = lax.broadcasted_iota(jnp.int32, (LANES, LANES), 0)
    spread = jnp.where(sub == 0, inverse, jnp.where(sub == 1, factor, 0.0)).T
    inverse_col = spread[0:per_block, 0:1]
    factor_col = spread[0:per_block, 1:2]

    rest = per_block - 2 * STRIP
    sends = (
        (0, STRIP, pl.ds(0, cols)),
        (STRIP, STRIP, pl.ds(0, cols)),
        (2 * STRIP, rest, pl.ds(0, half)),
        (2 * STRIP, rest, pl.ds(half, half)),
    )
    grads[mine, :] = (inverse_col * scaled[...] - factor_col * vals[...]).astype(BF16)
    grad_copies = []
    grad_sent = []

    def send_grads(g):
        at, size, span = sends[g]
        group = pl.ds(pl.multiple_of(d * per_block + at, 16), size)
        arrivals, sent = {}, []
        for step in order:
            to = {"dp": (d + step) % n_dp}
            sems = grad_send.at[g, step - 1], grad_recv.at[g, step - 1]
            copy = remote(grads.at[group, span], grads.at[group, span], *sems, to)
            copy.start()
            sent.append(copy.wait_send)
            source = (d + n_dp - step) % n_dp
            landed = grads.at[
                pl.ds(pl.multiple_of(source * per_block + at, 16), size), span
            ]
            arrivals[step] = remote(landed, landed, *sems, to)
        grad_copies.append(arrivals)
        grad_sent.append(sent)

    def grads_here(g):
        for copy in grad_copies[g].values():
            copy.wait_recv()

    def grads_gone(g):
        for wait in grad_sent[g]:
            wait()

    sib_copies = []

    def share_out(h):
        span = pl.ds(h * half, half)
        sib_out[h] = jnp.dot(
            xt[1 - core], grads[:, span], preferred_element_type=F32
        ).astype(BF16)
        copy = remote(
            sib_out.at[h],
            sib_in.at[h],
            sib_send.at[h],
            sib_recv.at[h],
            {"vis": v + 1 - 2 * core},
        )
        copy.start()
        sib_copies.append(copy)
        finish.append(copy.wait_send)

    def share_own(h):
        span = pl.ds(h * half, half)
        own_part[h] = jnp.dot(xt[core], grads[:, span], preferred_element_type=F32).astype(BF16)

    x_order = sorted(range(1, n_x), key=lambda s: -min(s, n_x - s))
    group_rows = STRIP * n_x

    def strip_row(g, at):
        if g == 0:
            row = d * per_block + at * STRIP
        elif g < 3:
            row = jnp.where(
                at == 0,
                d * per_block + group_rows + (g - 1) * STRIP,
                ((d + at) % n_dp) * per_block + (g - 1) * STRIP,
            )
        else:
            row = ((d + g - 2) % n_dp) * per_block + 2 * STRIP + at * STRIP
        return pl.ds(pl.multiple_of(row, 16), STRIP)

    def feature_products(g):
        group = jnp.concatenate([grads[strip_row(g, at), :] for at in range(n_x)], axis=0)
        row_part[pl.ds(g * group_rows, group_rows), :] = jnp.dot(
            group, wt[...], preferred_element_type=F32
        ).astype(BF16)
        copies = []
        for step in x_order:
            to = (xi + step) % n_x
            copy = remote(
                row_part.at[pl.ds(pl.multiple_of(g * group_rows + to * STRIP, 16), STRIP)],
                row_in.at[step - 1, pl.ds(g * STRIP, STRIP)],
                row_send.at[g, step - 1],
                row_recv.at[g, step - 1],
                {"tp": zh * n_x + to},
            )
            copy.start()
            copies.append(copy)
            finish.append(copy.wait_send)
        return copies

    def feature_cross(g, copies):
        inside = pl.ds(g * STRIP, STRIP)
        for copy in copies:
            copy.wait_recv()
        summed = row_part[
            pl.ds(pl.multiple_of(g * group_rows + xi * STRIP, 16), STRIP), :
        ].astype(F32)
        for step in range(1, n_x):
            summed = summed + row_in[step - 1, inside, :].astype(F32)
        cross_out[inside, :] = summed.astype(BF16)
        copy = remote(
            cross_out.at[inside],
            cross_in.at[inside],
            cross_send.at[g],
            cross_recv.at[g],
            {"tp": (t + n_x) % n_tp},
        )
        copy.start()
        finish.append(copy.wait_send)
        return copy

    def feature_spread(g, copy):
        inside = pl.ds(g * STRIP, STRIP)
        copy.wait_recv()
        place = strip_row(g, xi)
        fg_all[place, :] = (
            cross_out[inside, :].astype(F32) + cross_in[inside, :].astype(F32)
        ).astype(BF16)
        copies = []
        for step in x_order:
            to = {"tp": zh * n_x + (xi + step) % n_x}
            sems = full_send.at[g, step - 1], full_recv.at[g, step - 1]
            send = remote(fg_all.at[place], fg_all.at[place], *sems, to)
            send.start()
            finish.append(send.wait_send)
            landed = fg_all.at[strip_row(g, (xi + n_x - step) % n_x)]
            copies.append(remote(landed, landed, *sems, to))
        return copies

    def line_copy(out, into, send_sem, recv_sem, at, h, to):
        return remote(
            out.at[at, h], into.at[at, h], send_sem.at[at, h], recv_sem.at[at, h], {"vis": to}
        )

    right = jnp.minimum(v + 2, n_vis - 2 + core)
    left = jnp.maximum(v - 2, core)

    fine = half // FINE

    def pair_sum(at, q):
        span = pl.ds(pl.multiple_of(at * chunk, 16), chunk)
        h, inner = q // FINE, pl.ds(q % FINE * fine, fine)
        return own_part[h, span, inner].astype(F32) + sib_in[h, span, inner].astype(F32)

    def line_step(tau, halves=range(HALVES)):
        for h in [x * FINE + y for x in halves for y in range(FINE)]:

            @pl.when((z <= tau) & (z < n_z - 1) & (tau < n_z - 1))
            def _():
                at = n_z - 1 - tau + z
                copy = line_copy(right_out, right_in, right_send, right_recv, at, h, right)

                @pl.when(z > 0)
                def _():
                    copy.wait_recv()
                    right_out[at, h] = (
                        pair_sum(at, h) + right_in[at, h].astype(F32)
                    ).astype(BF16)

                @pl.when(z == 0)
                def _():
                    right_out[at, h] = pair_sum(at, h).astype(BF16)

                copy.start()

            @pl.when((n_z - 1 - z <= tau) & (z > 0) & (tau < n_z - 1))
            def _():
                at = tau - (n_z - 1 - z)
                copy = line_copy(left_out, left_in, left_send, left_recv, at, h, left)

                @pl.when(z < n_z - 1)
                def _():
                    copy.wait_recv()
                    left_out[at, h] = (
                        pair_sum(at, h) + left_in[at, h].astype(F32)
                    ).astype(BF16)

                @pl.when(z == n_z - 1)
                def _():
                    left_out[at, h] = pair_sum(at, h).astype(BF16)

                copy.start()

    def line_last():
        for h in range(HALVES * FINE):
            span = pl.ds(h * fine, fine)
            from_left = line_copy(right_out, right_in, right_send, right_recv, z, h, right)
            from_right = line_copy(left_out, left_in, left_send, left_recv, z, h, left)

            @pl.when(z > 0)
            def _():
                from_left.wait_recv()

            @pl.when(z < n_z - 1)
            def _():
                from_right.wait_recv()

            @pl.when(z == 0)
            def _():
                wg_ref[:, span] = (pair_sum(z, h) + left_in[z, h].astype(F32)).astype(BF16)

            @pl.when(z == n_z - 1)
            def _():
                wg_ref[:, span] = (pair_sum(z, h) + right_in[z, h].astype(F32)).astype(BF16)

            @pl.when((z > 0) & (z < n_z - 1))
            def _():
                wg_ref[:, span] = (
                    pair_sum(z, h) + right_in[z, h].astype(F32) + left_in[z, h].astype(F32)
                ).astype(BF16)

    def line_sent():
        for h in range(HALVES * FINE):

            def right_done(at, carry):
                line_copy(right_out, right_in, right_send, right_recv, at, h, right).wait_send()
                return carry

            def left_done(at, carry):
                line_copy(left_out, left_in, left_send, left_recv, at, h, left).wait_send()
                return carry

            lax.fori_loop(z + 1, n_z, right_done, 0)
            lax.fori_loop(0, z, left_done, 0)

    row_copies, cross, spread_copies = [], [], []
    send_grads(0)
    send_grads(1)
    row_copies.append(feature_products(0))
    grads_gone(0)
    send_grads(2)
    grads_here(0)
    row_copies.append(feature_products(1))
    cross.append(feature_cross(0, row_copies[0]))
    grads_gone(1)
    send_grads(3)
    grads_here(1)
    row_copies.append(feature_products(2))
    cross.append(feature_cross(1, row_copies[1]))
    grads_here(2)
    share_out(0)
    share_own(0)
    cross.append(feature_cross(2, row_copies[2]))
    sib_copies[0].wait_recv()
    line_step(0, (0,))
    grads_here(3)
    share_out(1)
    share_own(1)
    row_copies.append(feature_products(3))
    row_copies.append(feature_products(4))
    row_copies.append(feature_products(5))
    sib_copies[1].wait_recv()
    line_step(0, (1,))
    spread_copies += feature_spread(0, cross[0])
    cross.append(feature_cross(3, row_copies[3]))
    spread_copies += feature_spread(1, cross[1])
    line_step(1)
    cross.append(feature_cross(4, row_copies[4]))
    spread_copies += feature_spread(2, cross[2])
    cross.append(feature_cross(5, row_copies[5]))
    line_step(2)
    spread_copies += feature_spread(3, cross[3])
    line_step(3)
    spread_copies += feature_spread(4, cross[4])
    line_step(4)
    spread_copies += feature_spread(5, cross[5])
    line_step(5)
    for copy in spread_copies:
        copy.wait_recv()
    pieces = store_sems.shape[0]
    size = rows // pieces
    stores = [
        pltpu.make_async_copy(
            fg_all.at[pl.ds(k * size, size)], fg_ref.at[pl.ds(k * size, size)], store_sems.at[k]
        )
        for k in range(pieces)
    ]
    for store in stores:
        store.start()
    line_step(6)
    line_last()
    for store in stores:
        store.wait()
    line_sent()
    grads_gone(2)
    grads_gone(3)
    for wait in finish:
        wait()


def hand_on(fg_in, wg_in, fg_ref, wg_ref, fg_held, wg_held, sems_in, sems_out):
    pieces = sems_in.shape[0] - 1
    size = fg_in.shape[0] // pieces
    spans = [pl.ds(at * size, size) for at in range(pieces)]
    sources = [fg_in.at[span] for span in spans] + [wg_in]
    held = [fg_held.at[span] for span in spans] + [wg_held]
    targets = [fg_ref.at[span] for span in spans] + [wg_ref]
    into = [pltpu.make_async_copy(a, b, sems_in.at[k]) for k, (a, b) in enumerate(zip(sources, held))]
    out = [pltpu.make_async_copy(a, b, sems_out.at[k]) for k, (a, b) in enumerate(zip(held, targets))]
    for copy in into:
        copy.start()
    for first, second in zip(into, out):
        first.wait()
        second.start()
    for copy in out:
        copy.wait()


def on_device(features, merge_weight, gain, positions, cotangent):
    rows, sub_count, width = features.shape
    cols = merge_weight.shape[2]
    n_vis, n_tp, n_dp = (lax.axis_size(name) for name in ("vis", "tp", "dp"))
    blocks = n_vis * n_dp
    per_block = rows // n_dp
    slots_dev = cotangent.shape[0]
    groups = cols // LANES
    tile = CAP * groups
    n_x, n_z = n_tp // 2, n_vis // 2
    half = cols // HALVES
    chunk = width // n_vis
    share = width // 2
    part_rows = rows // n_x
    n_groups = part_rows // STRIP
    vmem = pl.BlockSpec(memory_space=pltpu.VMEM)
    anywhere = pl.BlockSpec(memory_space=pl.ANY)
    dma = pltpu.SemaphoreType.DMA
    feature_grad, weight_grad = pl.pallas_call(
        functools.partial(kernel, (n_vis, n_tp, n_dp)),
        out_shape=(
            jax.ShapeDtypeStruct((rows, width), BF16),
            jax.ShapeDtypeStruct((chunk, cols), BF16),
        ),
        in_specs=[anywhere] * 2 + [vmem] * 3,
        out_specs=(anywhere, vmem),
        scratch_shapes=[
            pltpu.VMEM((rows, width), BF16),
            pltpu.VMEM((width, cols), BF16),
            pltpu.VMEM((blocks * tile, LANES), F32),
            pltpu.VMEM((blocks, tile, LANES), BF16),
            pltpu.VMEM((blocks, tile, LANES), BF16),
            pltpu.VMEM((rows, cols), BF16),
            pltpu.VMEM((n_dp - 1, per_block, cols), BF16),
            pltpu.VMEM((per_block, cols), F32),
            pltpu.VMEM((per_block, cols), F32),
            pltpu.VMEM((LANES, LANES), F32),
            pltpu.VMEM((8, LANES), F32),
            pltpu.VMEM((n_tp, 8, LANES), F32),
            pltpu.VMEM((rows, cols), BF16),
            pltpu.VMEM((width, rows), BF16),
            pltpu.VMEM((2, share, rows), BF16),
            pltpu.VMEM((cols, width), BF16),
            pltpu.VMEM((HALVES, share, half), BF16),
            pltpu.VMEM((HALVES, share, half), BF16),
            pltpu.VMEM((HALVES, share, half), BF16),
            pltpu.VMEM((n_z, HALVES * FINE, chunk, half // FINE), BF16),
            pltpu.VMEM((n_z, HALVES * FINE, chunk, half // FINE), BF16),
            pltpu.VMEM((n_z, HALVES * FINE, chunk, half // FINE), BF16),
            pltpu.VMEM((n_z, HALVES * FINE, chunk, half // FINE), BF16),
            pltpu.VMEM((rows, width), BF16),
            pltpu.VMEM((n_x - 1, part_rows, width), BF16),
            pltpu.VMEM((part_rows, width), BF16),
            pltpu.VMEM((part_rows, width), BF16),
            pltpu.VMEM((rows, width), BF16),
            dma,
            dma,
            dma((HALVES, n_dp - 1)),
            dma((HALVES, n_dp - 1)),
            dma((n_tp - 1,)),
            dma((n_tp - 1,)),
            dma((SENDS, n_dp - 1)),
            dma((SENDS, n_dp - 1)),
            dma((HALVES,)),
            dma((HALVES,)),
            dma((n_z, HALVES * FINE)),
            dma((n_z, HALVES * FINE)),
            dma((n_z, HALVES * FINE)),
            dma((n_z, HALVES * FINE)),
            dma((n_groups, n_x - 1)),
            dma((n_groups, n_x - 1)),
            dma((n_groups,)),
            dma((n_groups,)),
            dma((n_groups, n_x - 1)),
            dma((n_groups, n_x - 1)),
            dma((2,)),
            dma((n_groups,)),
        ],
        compiler_params=pltpu.CompilerParams(
            collective_id=0, has_side_effects=True, vmem_limit_bytes=56 << 20
        ),
        cost_estimate=pl.CostEstimate(
            flops=6 * rows * width * cols, bytes_accessed=6 * width * cols, transcendentals=LANES
        ),
    )(
        features.reshape(rows, width),
        merge_weight.reshape(width, cols),
        gain.reshape(1, cols),
        positions.reshape(-1, LANES),
        cotangent,
    )
    feature_grad, weight_grad = pl.pallas_call(
        hand_on,
        out_shape=(
            jax.ShapeDtypeStruct((rows, width), BF16),
            jax.ShapeDtypeStruct((chunk, cols), BF16),
        ),
        in_specs=[anywhere] * 2,
        out_specs=(anywhere, anywhere),
        scratch_shapes=[
            pltpu.VMEM((rows, width), BF16),
            pltpu.VMEM((chunk, cols), BF16),
            dma((PIECES + 1,)),
            dma((PIECES + 1,)),
        ],
        compiler_params=pltpu.CompilerParams(vmem_limit_bytes=60 << 20),
    )(feature_grad, weight_grad)
    return (feature_grad.reshape(features.shape), weight_grad.reshape(1, chunk, cols))


def solution(mesh):
    return jax.shard_map(
        on_device,
        mesh=mesh,
        in_specs=(P("vis", "dp", None), P("dp", None, "tp"), P("tp"), P(), P(("vis", "dp"), "tp")),
        out_specs=(P("vis", "dp", None), P("dp", "vis", "tp")),
        check_vma=False,
    )
```
